32 devices in a mesh: band: 8 (over z, y), patch: 4 (over x, core).
Axes of the slice: x: 2, y: 2, z: 4, core: 2. Of those that a mesh axis runs over, the one named last changes fastest.
Arguments:
- grid_state: bfloat16 [32, 1024, 512], P('band', 'patch'), may hold values from -6 to 6
- mesh_state: bfloat16 [8, 4, 256, 512], P('band', 'patch'), may hold values from -6 to 6
- g2m_features: bfloat16 [8, 4, 2048, 512], P('band', 'patch'), may hold values from -6 to 6
- g2m_sender: int32 [8, 4, 2048], P('band', 'patch'), may hold values from 0 to 2079, as said below
- g2m_receiver: int32 [8, 4, 2048], P('band', 'patch'), may hold values from 0 to 255
- g2m_blocks: int32 [8, 4], replicated, may hold values from 4 to 16, as said below
- proc_features: bfloat16 [8, 4, 2048, 512], P('band', 'patch'), may hold values from -6 to 6
- proc_sender: int32 [8, 4, 2048], P('band', 'patch'), may hold values from 0 to 2815, as said below
- proc_receiver: int32 [8, 4, 2048], P('band', 'patch'), may hold values from 0 to 255
- dec_features: bfloat16 [3, 32, 1024, 512], P(None, 'band', 'patch'), may hold values from -6 to 6
- dec_sender: int32 [3, 32, 1024], P(None, 'band', 'patch'), may hold values from 0 to 2111, as said below
- enc_weights: bfloat16 [9, 512, 512], replicated, may hold values from -0.25 to 0.25
- proc_weights: bfloat16 [7, 512, 512], replicated, may hold values from -0.25 to 0.25
- dec_weights: bfloat16 [7, 512, 512], replicated, may hold values from -0.25 to 0.25
Outputs:
- grid_out: bfloat16 [32, 1024, 512], P('band', 'patch')
The draws below stay inside these ranges and needn't reach their ends.
Inputs may be any that keep to these rules, and one draw needn't show every extreme that they name: `g2m_blocks`: the bands at both poles hold 16 live blocks in every sector. `g2m_sender`: never a latitude row before the first or after the last of the grid. `proc_sender`: below 2304, s % 256 is below 64 unless s // 256 = 4; never a band before the first or after the last. `dec_sender`: s % 256 is below 64 unless s // 256 = 4; never a band before the first or after the last.
All inputs are finite; a program needn't handle non-finite values.
Results may differ from the reference program's by a relative error of at most 0.0095.
Values may be sent and summed in bfloat16 or wider, within the bound.
A program may use at most 128 MiB of HBM per device.

```python
import jax
import jax.numpy as jnp
from jax import lax

D = 512
LAT_DEV = 4
LON_DEV = 256
MESH_DEV = 256
COARSE_DEV = 16
G2M_DEV = 2048
PROC_DEV = 2048
HALO = 2
BORDER = 64
G2M_BLK = 16
BANDS = 8
PATCHES = 4
NLAT = 32
NLON = 1024
COARSE = 512


def neighbour_slots(key, band_index, dims_shape, border_rows):
    pick_key, row_key = jax.random.split(key)
    pick_draw = jax.random.randint(pick_key, dims_shape, 0, 8, dtype=jnp.int32)
    neighbour = pick_draw + (pick_draw >= 4).astype(jnp.int32)
    neighbour = jnp.where((band_index == 0) & (neighbour < 3), neighbour + 6, neighbour)
    neighbour = jnp.where((band_index == BANDS - 1) & (neighbour >= 6), neighbour - 6, neighbour)
    row_draw = jax.random.randint(row_key, dims_shape, 0, border_rows, dtype=jnp.int32)
    return neighbour * MESH_DEV + row_draw


def draw_g2m_blocks(key, part):
    key = jax.random.fold_in(key, 11)
    band_index = jnp.arange(BANDS, dtype=jnp.int32)[:, None]
    distance = jnp.minimum(band_index, BANDS - 1 - band_index)
    jitter_top = max(2, G2M_BLK // 4 + 1)
    jitter = jax.random.randint(key, (BANDS, PATCHES), 0, jitter_top, dtype=jnp.int32) * (distance > 0).astype(jnp.int32)
    block_count = G2M_BLK - 3 * distance * G2M_BLK // BANDS - jitter
    return jnp.clip(block_count, max(1, G2M_BLK // 4), G2M_BLK).astype(jnp.int32)


def draw_g2m_sender(key, part):
    key = jax.random.fold_in(key, 12)
    row_key, col_key = jax.random.split(key)
    padded_width = LON_DEV + 2 * HALO
    dims_shape = (BANDS, PATCHES, G2M_DEV)
    band_index = jnp.arange(BANDS, dtype=jnp.int32)[:, None, None]
    low_row = jnp.where(band_index == 0, HALO, 0)
    high_row = jnp.where(band_index == BANDS - 1, LAT_DEV + HALO, LAT_DEV + 2 * HALO)
    row_draw = jax.random.randint(row_key, dims_shape, 0, 1 << 20, dtype=jnp.int32)
    row_draw = low_row + row_draw % (high_row - low_row)
    col_draw = jax.random.randint(col_key, dims_shape, 0, padded_width, dtype=jnp.int32)
    sender = row_draw * padded_width + col_draw
    sender = sender.at[1, 0, 0].set((LAT_DEV + 2 * HALO) * padded_width - 1)
    sender = sender.at[1, 0, 1].set(0)
    return sender.astype(jnp.int32)


def draw_g2m_receiver(key, part):
    key = jax.random.fold_in(key, 13)
    receiver = jax.random.randint(key, (BANDS, PATCHES, G2M_DEV), 0, MESH_DEV, dtype=jnp.int32)
    receiver = receiver.at[0, 0, 0].set(MESH_DEV - 1)
    receiver = receiver.at[0, 0, 1].set(0)
    return receiver


def draw_proc_sender(key, part):
    key = jax.random.fold_in(key, 14)
    kind_key, near_key, own_key, far_key = jax.random.split(key, 4)
    dims_shape = (BANDS, PATCHES, PROC_DEV)
    band_index = jnp.arange(BANDS, dtype=jnp.int32)[:, None, None]
    kind_draw = jax.random.randint(kind_key, dims_shape, 0, 8, dtype=jnp.int32)
    nearby = neighbour_slots(near_key, band_index, dims_shape, BORDER)
    own_rows = 4 * MESH_DEV + jax.random.randint(own_key, dims_shape, 0, MESH_DEV, dtype=jnp.int32)
    distant = 9 * MESH_DEV + jax.random.randint(far_key, dims_shape, 0, COARSE, dtype=jnp.int32)
    sender = jnp.where(kind_draw < 2, distant, jnp.where(kind_draw < 5, own_rows, nearby))
    sender = sender.at[1, 0, 0].set(9 * MESH_DEV + COARSE - 1)
    sender = sender.at[1, 0, 1].set(0)
    sender = sender.at[1, 0, 2].set(BORDER - 1)
    return sender.astype(jnp.int32)


def draw_proc_receiver(key, part):
    key = jax.random.fold_in(key, 15)
    receiver = jax.random.randint(key, (BANDS, PATCHES, PROC_DEV), 0, MESH_DEV, dtype=jnp.int32)
    receiver = receiver.at[0, 0, 0].set(MESH_DEV - 1)
    receiver = receiver.at[0, 0, 1].set(0)
    return receiver


def draw_dec_sender(key, part):
    key = jax.random.fold_in(key, 16)
    kind_key, near_key, own_key = jax.random.split(key, 3)
    dims_shape = (3, NLAT, NLON)
    band_index = (jnp.arange(NLAT, dtype=jnp.int32) // LAT_DEV)[None, :, None]
    kind_draw = jax.random.randint(kind_key, dims_shape, 0, 2, dtype=jnp.int32)
    nearby = neighbour_slots(near_key, band_index, dims_shape, BORDER)
    own_rows = 4 * MESH_DEV + jax.random.randint(own_key, dims_shape, 0, MESH_DEV, dtype=jnp.int32)
    sender = jnp.where(kind_draw == 0, own_rows, nearby)
    sender = sender.at[0, LAT_DEV, 0].set(8 * MESH_DEV + BORDER - 1)
    sender = sender.at[1, LAT_DEV, 0].set(0)
    return sender.astype(jnp.int32)


def levels(key, extent, cuts, smallest, top_value):
    loudness, own = 1.0, jax.random.fold_in(key, 6)
    for axis_at, blocks in cuts:
        draws = jnp.exp(jax.random.uniform(jax.random.fold_in(own, axis_at), (blocks,), jnp.float32, smallest / len(cuts), top_value / len(cuts)))
        loudness = loudness * jnp.repeat(draws, extent[axis_at] // blocks).reshape([-1 if axis == axis_at else 1 for axis in range(len(extent))])
    return loudness


def gaussian(key, shape, deviation, bound, cuts=(), kind=jnp.bfloat16):
    values = deviation * jax.random.normal(key, shape, jnp.float32)
    if cuts:
        values = values * levels(key, shape, cuts, -0.22, 0.18)
    return jnp.clip(values, -bound, bound).astype(kind)


def setup_inputs(seed: int = 0) -> dict:
    streams_of = jax.random.split(jax.random.key(seed), 15)
    return {
        "grid_state": gaussian(streams_of[0], (NLAT, NLON, D), 1.0, 6.0, ((0, 8), (1, 4))),
        "mesh_state": gaussian(streams_of[1], (BANDS, PATCHES, MESH_DEV, D), 1.0, 6.0, ((0, 8), (1, 4))),
        "g2m_features": gaussian(streams_of[2], (BANDS, PATCHES, G2M_DEV, D), 1.0, 6.0, ((0, 8), (1, 4))),
        "g2m_sender": draw_g2m_sender(jax.random.fold_in(streams_of[14], 71), 0),
        "g2m_receiver": draw_g2m_receiver(jax.random.fold_in(streams_of[14], 71), 0),
        "g2m_blocks": draw_g2m_blocks(jax.random.fold_in(streams_of[14], 71), 0),
        "proc_features": gaussian(streams_of[6], (BANDS, PATCHES, PROC_DEV, D), 1.0, 6.0, ((0, 8), (1, 4))),
        "proc_sender": draw_proc_sender(jax.random.fold_in(streams_of[14], 71), 0),
        "proc_receiver": draw_proc_receiver(jax.random.fold_in(streams_of[14], 71), 0),
        "dec_features": gaussian(streams_of[9], (3, NLAT, NLON, D), 1.0, 6.0, ((1, 8), (2, 4))),
        "dec_sender": draw_dec_sender(jax.random.fold_in(streams_of[14], 71), 0),
        "enc_weights": gaussian(streams_of[11], (9, D, D), D ** -0.5, 0.25),
        "proc_weights": gaussian(streams_of[12], (7, D, D), D ** -0.5, 0.25),
        "dec_weights": gaussian(streams_of[13], (7, D, D), D ** -0.5, 0.25),
    }


epsilon = 1e-05

def layer_norm(values):
    average = lax.optimization_barrier(jnp.mean(values, axis=-1, keepdims=True))
    centred = values - average
    spread = lax.optimization_barrier(jnp.mean(centred * centred, axis=-1, keepdims=True))
    return centred * lax.rsqrt(spread + epsilon)

def project(values, weight):
    matrix = values.reshape(-1, values.shape[-1])
    result = jnp.dot(matrix, weight, preferred_element_type=jnp.float32)
    return result.reshape(values.shape[:-1] + (weight.shape[1],))

def edge_message(features, send_rows, recv_rows, w_edge, w_out):
    before = project(features, w_edge) + send_rows.astype(jnp.float32) + recv_rows.astype(jnp.float32)
    hidden = jax.nn.silu(before).astype(jnp.bfloat16)
    return layer_norm(project(hidden, w_out)).astype(jnp.bfloat16)

def node_update(current, summed, w_self, w_total, w_out):
    before = project(current, w_self) + project(summed.astype(jnp.bfloat16), w_total)
    hidden = jax.nn.silu(before).astype(jnp.bfloat16)
    return (current.astype(jnp.float32) + layer_norm(project(hidden, w_out))).astype(jnp.bfloat16)

def self_update(current, w_first, w_out):
    hidden = jax.nn.silu(project(current, w_first)).astype(jnp.bfloat16)
    return (current.astype(jnp.float32) + layer_norm(project(hidden, w_out))).astype(jnp.bfloat16)

def close_rows(source, band_index, patch_index, sender):
    neighbour = sender // MESH_DEV
    src_band = (band_index + neighbour // 3 - 1) % BANDS
    src_patch = (patch_index + neighbour % 3 - 1) % PATCHES
    return source[src_band, src_patch, sender % MESH_DEV]

def reference(grid_state, mesh_state, g2m_features, g2m_sender, g2m_receiver, g2m_blocks, proc_features, proc_sender, proc_receiver, dec_features, dec_sender, enc_weights, proc_weights, dec_weights):
    padded_width = LON_DEV + 2 * HALO
    grid_send = project(grid_state, enc_weights[0]).astype(jnp.bfloat16)
    mesh_recv = project(mesh_state, enc_weights[1]).astype(jnp.bfloat16)
    wrapped = jnp.concatenate([grid_send[:, NLON - HALO:], grid_send, grid_send[:, :HALO]], axis=1)
    lat_rim = jnp.zeros((HALO, NLON + 2 * HALO, D), grid_send.dtype)
    padded = jnp.concatenate([lat_rim, wrapped, lat_rim], axis=0)
    devices = jnp.arange(BANDS * PATCHES, dtype=jnp.int32)

    def encode(device):
        band_index = device // PATCHES
        patch_index = device % PATCHES
        sender = g2m_sender[band_index, patch_index]
        receiver = g2m_receiver[band_index, patch_index]
        send_rows = padded[band_index * LAT_DEV + sender // padded_width, patch_index * LON_DEV + sender % padded_width]
        recv_rows = mesh_recv[band_index, patch_index][receiver]
        message = edge_message(g2m_features[band_index, patch_index], send_rows, recv_rows, enc_weights[2], enc_weights[3])
        live_mask = jnp.arange(G2M_DEV, dtype=jnp.int32) // 128 < g2m_blocks[band_index, patch_index]
        message = jnp.where(live_mask[:, None], message, jnp.zeros_like(message))
        return jax.ops.segment_sum(message.astype(jnp.float32), receiver, num_segments=MESH_DEV)
    enc_total = lax.map(encode, devices).reshape(BANDS, PATCHES, MESH_DEV, D)
    mesh_next = node_update(mesh_state, enc_total, enc_weights[4], enc_weights[5], enc_weights[6])
    grid_next = self_update(grid_state, enc_weights[7], enc_weights[8])
    proc_send = project(mesh_next, proc_weights[0]).astype(jnp.bfloat16)
    proc_recv = project(mesh_next, proc_weights[1]).astype(jnp.bfloat16)
    coarse = proc_send[:, :, MESH_DEV - COARSE_DEV:].reshape(COARSE, D)

    def process(device):
        band_index = device // PATCHES
        patch_index = device % PATCHES
        sender = proc_sender[band_index, patch_index]
        receiver = proc_receiver[band_index, patch_index]
        nearby = close_rows(proc_send, band_index, patch_index, jnp.minimum(sender, 9 * MESH_DEV - 1))
        distant = coarse[jnp.clip(sender - 9 * MESH_DEV, 0, COARSE - 1)]
        send_rows = jnp.where((sender < 9 * MESH_DEV)[:, None], nearby, distant)
        recv_rows = proc_recv[band_index, patch_index][receiver]
        message = edge_message(proc_features[band_index, patch_index], send_rows, recv_rows, proc_weights[2], proc_weights[3])
        return jax.ops.segment_sum(message.astype(jnp.float32), receiver, num_segments=MESH_DEV)
    proc_total = lax.map(process, devices).reshape(BANDS, PATCHES, MESH_DEV, D)
    mesh_last = node_update(mesh_next, proc_total, proc_weights[4], proc_weights[5], proc_weights[6])
    dec_send = project(mesh_last, dec_weights[0]).astype(jnp.bfloat16)
    dec_recv = project(grid_next, dec_weights[1]).astype(jnp.bfloat16)
    cell_band = (jnp.arange(NLAT, dtype=jnp.int32) // LAT_DEV)[:, None]
    cell_patch = (jnp.arange(NLON, dtype=jnp.int32) // LON_DEV)[None, :]
    dec_total = jnp.zeros((NLAT, NLON, D), jnp.float32)
    for which in range(3):
        send_rows = close_rows(dec_send, cell_band, cell_patch, dec_sender[which])
        message = edge_message(dec_features[which], send_rows, dec_recv, dec_weights[2], dec_weights[3])
        dec_total = dec_total + message.astype(jnp.float32)
    return node_update(grid_next, dec_total, dec_weights[4], dec_weights[5], dec_weights[6])
```

```python
import functools

import jax
import jax.numpy as jnp
from jax import lax
from jax.experimental import pallas as pl
from jax.experimental.pallas import tpu as pltpu
from jax.sharding import PartitionSpec as P

MESH = pl.DeviceIdType.MESH
COARSE_DEV = 16
HALO = 2
BORDER = 64
EPSILON = 1e-05
BF = jnp.bfloat16
F32 = jnp.float32
ROWS = 512

G_NORTH, G_SOUTH, G_WEST, G_EAST = 0, 3, 6, 7
G_FORWARD = 8
P_SIDE, P_FORWARD, D_SIDE, D_FORWARD = 12, 16, 20, 24
C_BASE = 28


def dot(a, b):
    return jnp.dot(a, b, preferred_element_type=F32)


def silu(v):
    half = 0.5 * v
    return half + half * jnp.tanh(half)


def layer_norm(v):
    centred = v - jnp.mean(v, axis=-1, keepdims=True)
    spread = jnp.mean(centred * centred, axis=-1, keepdims=True)
    return centred * lax.rsqrt(spread + EPSILON)


def columns_of(row):
    n = row.shape[1]
    wide = jnp.broadcast_to(row.astype(F32), (128, n)).T
    return wide.astype(jnp.int32).astype(jnp.int16)


def pick(columns, first, count):
    lane = lax.broadcasted_iota(jnp.int16, columns.shape, 1)
    parts = []
    for start in range(first, first + count, 128):
        hit = columns == lane + jnp.int16(start)
        parts.append(jnp.where(hit, BF(1), BF(0)))
    return jnp.concatenate(parts, axis=1) if len(parts) > 1 else parts[0]


def scatter(row, nodes):
    hit = lax.broadcasted_iota(jnp.int32, (nodes, row.shape[1]), 0) == row
    return jnp.where(hit, 1.0, 0.0).astype(BF)


def body(
    bands,
    patches,
    grid_in,
    mesh_in,
    gfeat_in,
    gsend_in,
    grecv_in,
    blocks,
    pfeat_in,
    psend_in,
    precv_in,
    dfeat_in,
    dsend_in,
    encw_in,
    procw_in,
    decw_in,
    out,
    grid,
    mesh,
    gfeat,
    gsend,
    grecv,
    pfeat,
    psend,
    precv,
    dfeat,
    dsend,
    encw,
    procw,
    decw,
    table,
    mrecv,
    gnext,
    pre_g,
    pre_p,
    pre_d,
    upd,
    total,
    mnext,
    pown,
    pnear,
    pcoarse,
    precv_rows,
    down,
    dnear,
    result,
    in_sem,
    out_sem,
    send_sem,
    recv_sem,
):
    band, patch = lax.axis_index("band"), lax.axis_index("patch")
    has_north, has_south = band > 0, band < bands - 1
    west, east = lax.rem(patch + patches - 1, patches), lax.rem(patch + 1, patches)
    lat, lon, latent = grid.shape
    nodes = mesh.shape[0]
    half_lat = ROWS // lon

    loads = {}

    def load(name, src, dst):
        copy = pltpu.make_async_copy(src, dst, in_sem.at[len(loads)])
        copy.start()
        loads[name] = copy

    load("grid", grid_in, grid)
    load("e0", encw_in.at[0], encw.at[0])
    load("e78", encw_in.at[pl.ds(7, 2)], encw.at[pl.ds(7, 2)])
    load("mesh", mesh_in.at[0, 0], mesh)
    load("e12", encw_in.at[pl.ds(1, 2)], encw.at[pl.ds(1, 2)])
    load("gs", gsend_in.at[0], gsend)
    load("gr", grecv_in.at[0], grecv)
    load("gf", gfeat_in.at[0, 0], gfeat)
    load("p2", procw_in.at[2], procw.at[2])
    load("pf", pfeat_in.at[0, 0], pfeat)
    load("e36", encw_in.at[pl.ds(3, 4)], encw.at[pl.ds(3, 4)])
    load("p01", procw_in.at[pl.ds(0, 2)], procw.at[pl.ds(0, 2)])
    load("ps", psend_in.at[0], psend)
    load("pr", precv_in.at[0], precv)
    load("d", decw_in, decw)
    load("df", dfeat_in, dfeat)
    load("ds", dsend_in, dsend)
    load("p36", procw_in.at[pl.ds(3, 4)], procw.at[pl.ds(3, 4)])

    def need(*names):
        for name in names:
            loads[name].wait()

    barrier = pltpu.get_barrier_semaphore()
    for k in range(1, bands):
        pl.semaphore_signal(
            barrier, inc=1, device_id={"band": lax.rem(band + k, bands), "patch": patch}, device_id_type=MESH
        )
    greeted = [k for k in range(1, patches) if k in (1, patches - 1) or k % 2 == 0]
    for k in greeted:
        pl.semaphore_signal(
            barrier, inc=1, device_id={"band": band, "patch": lax.rem(patch + k, patches)}, device_id_type=MESH
        )

    def remote(src, dst, number, to_band, to_patch):
        return pltpu.make_async_remote_copy(
            src_ref=src,
            dst_ref=dst,
            send_sem=send_sem.at[number],
            recv_sem=recv_sem.at[number],
            device_id={"band": to_band, "patch": to_patch},
            device_id_type=MESH,
        )

    @pl.when(jnp.logical_not(has_north))
    def _():
        table[4:6] = jnp.zeros_like(table[4:6])
        table[8, 8:12] = jnp.zeros_like(table[8, 8:12])
        pnear[0:3] = jnp.zeros_like(pnear[0:3])
        dnear[0:3] = jnp.zeros_like(dnear[0:3])

    @pl.when(jnp.logical_not(has_south))
    def _():
        table[6:8] = jnp.zeros_like(table[6:8])
        table[8, 12:16] = jnp.zeros_like(table[8, 12:16])
        pnear[5:8] = jnp.zeros_like(pnear[5:8])
        dnear[5:8] = jnp.zeros_like(dnear[5:8])

    groups = lon // 16
    north_band, south_band = lax.rem(band + bands - 1, bands), lax.rem(band + 1, bands)
    cuts = ((0, 1), (groups - 1, 1), (1, groups - 2))
    g_north = [
        remote(
            table.at[pl.ds(0, 2), pl.ds(a, n)], table.at[pl.ds(6, 2), pl.ds(a, n)], G_NORTH + i, north_band, patch
        )
        for i, (a, n) in enumerate(cuts)
    ]
    g_south = [
        remote(
            table.at[pl.ds(2, 2), pl.ds(a, n)], table.at[pl.ds(4, 2), pl.ds(a, n)], G_SOUTH + i, south_band, patch
        )
        for i, (a, n) in enumerate(cuts)
    ]
    g_west = remote(table.at[pl.ds(0, 4), 0], table.at[8, pl.ds(4, 4)], G_WEST, band, west)
    g_east = remote(table.at[pl.ds(0, 4), groups - 1], table.at[8, pl.ds(0, 4)], G_EAST, band, east)
    g_north_on = [
        remote(table.at[pl.ds(4, 2), 0], table.at[8, pl.ds(10, 2)], G_FORWARD, band, west),
        remote(table.at[pl.ds(4, 2), groups - 1], table.at[8, pl.ds(8, 2)], G_FORWARD + 1, band, east),
    ]
    g_south_on = [
        remote(table.at[pl.ds(6, 2), 0], table.at[8, pl.ds(14, 2)], G_FORWARD + 2, band, west),
        remote(table.at[pl.ds(6, 2), groups - 1], table.at[8, pl.ds(12, 2)], G_FORWARD + 3, band, east),
    ]

    def near_copies(own, near, side, forward):
        rows = own.at[pl.ds(0, BORDER)]
        north = remote(rows, near.at[6], side, north_band, patch)
        south = remote(rows, near.at[1], side + 1, south_band, patch)
        flat = [remote(rows, near.at[4], side + 2, band, west), remote(rows, near.at[3], side + 3, band, east)]
        north_on = [
            remote(near.at[1], near.at[2], forward, band, west),
            remote(near.at[1], near.at[0], forward + 1, band, east),
        ]
        south_on = [
            remote(near.at[6], near.at[7], forward + 2, band, west),
            remote(near.at[6], near.at[5], forward + 3, band, east),
        ]
        return [north], [south], flat, north_on, south_on

    def when_all(condition, copies, method):
        @pl.when(condition)
        def _():
            for copy in copies:
                getattr(copy, method)()

    def start_sides(north, south, flat):
        when_all(has_north, north, "start")
        when_all(has_south, south, "start")
        for copy in flat:
            copy.start()

    def pass_on(from_south, from_north, north_on, south_on):
        when_all(has_north, from_north, "wait_recv")
        when_all(has_north, north_on, "start")
        when_all(has_south, from_south, "wait_recv")
        when_all(has_south, south_on, "start")

    def finish(north, south, flat, north_on, south_on):
        for copy in flat:
            copy.wait_recv()
        when_all(has_north, north_on, "wait_recv")
        when_all(has_south, south_on, "wait_recv")
        when_all(has_north, north, "wait_send")
        when_all(has_south, south, "wait_send")
        for copy in flat:
            copy.wait_send()
        when_all(has_north, north_on, "wait_send")
        when_all(has_south, south_on, "wait_send")

    def loop(count, step):
        def one(i, carry):
            step(i)
            return carry

        lax.fori_loop(0, count, one, 0)

    def at(i):
        return pl.ds(pl.multiple_of(i * ROWS, ROWS), ROWS)

    grid_steps = lat * lon // ROWS

    def grid_rows(i):
        return grid[pl.ds(i * half_lat, half_lat)].reshape(ROWS, latent)

    need("grid", "e0")

    def send_step(i):
        rows = dot(grid_rows(i), encw[0]).astype(BF)
        table[pl.ds(i * half_lat, half_lat)] = rows.reshape(half_lat, groups, 16, latent)

    loop(grid_steps, send_step)
    pl.semaphore_wait(barrier, bands - 1 + len(greeted))
    start_sides(g_north, g_south, [g_west, g_east])

    need("e78")

    def self_step(i):
        rows = grid_rows(i)
        hidden = silu(dot(rows, encw[7])).astype(BF)
        gnext[at(i)] = (rows.astype(F32) + layer_norm(dot(hidden, encw[8]))).astype(BF)

    loop(grid_steps, self_step)
    need("mesh", "e12")
    mrecv[...] = dot(mesh[...], encw[1]).astype(BF)
    pass_on(g_north[:2], g_south[:2], g_north_on, g_south_on)

    width = lon + 2 * HALO

    def grid_place(s):
        i = jnp.zeros_like(s)
        for k in range(1, lat + 2 * HALO):
            i = i + (s >= k * width).astype(jnp.int32)
        j = s - i * width
        north, south = i < HALO, i >= lat + HALO
        line = jnp.where(north, i + 4, jnp.where(south, i, i - 2))
        inner = line * lon + j - HALO
        left = jnp.where(north, i + 8, jnp.where(south, i + 6, i - 2)) * 16 + j + 14
        right = jnp.where(north, i + 10, jnp.where(south, i + 8, i + 2)) * 16 + j - (lon + HALO)
        edge = 8 * lon + jnp.where(j < HALO, left, right)
        return jnp.where((j < HALO) | (j >= lon + HALO), edge, inner)

    need("gs", "gr", "gf")

    def enc_own(i):
        place = columns_of(grid_place(gsend[:, at(i)]))
        recv = columns_of(grecv[:, at(i)])
        left = jnp.concatenate([gfeat[at(i)], pick(place, 0, 4 * lon), pick(recv, 0, nodes)], axis=1)
        right = jnp.concatenate([encw[2], table[0:4].reshape(4 * lon, latent), mrecv[...]], axis=0)
        pre_g[at(i)] = dot(left, right)

    loop(gfeat.shape[0] // ROWS, enc_own)
    need("p2", "pf")

    def proc_feat(i):
        pre_p[at(i)] = dot(pfeat[at(i)], procw[2])

    loop(pfeat.shape[0] // ROWS, proc_feat)
    need("d", "df", "ds")

    def dec_part(i):
        recv = dot(gnext[at(i)], decw[1]).astype(BF).astype(F32)
        for k in range(3):
            rows = dfeat[k, pl.ds(i * half_lat, half_lat)].reshape(ROWS, latent)
            pre_d[k, at(i)] = dot(rows, decw[2]) + recv

    loop(grid_steps, dec_part)

    when_all(has_south, g_north[2:], "wait_recv")
    when_all(has_north, g_south[2:], "wait_recv")
    finish(g_north, g_south, [g_west, g_east], g_north_on, g_south_on)
    need("e36")
    total[...] = jnp.zeros_like(total)
    live = blocks[band, patch] * 128

    def enc_edges(i):
        place = columns_of(grid_place(gsend[:, at(i)]))
        before = pre_g[at(i)] + dot(pick(place, 4 * lon, 5 * lon), table[4:9].reshape(5 * lon, latent))
        message = layer_norm(dot(silu(before).astype(BF), encw[3])).astype(BF)
        edge = lax.broadcasted_iota(jnp.int32, (1, ROWS), 1) + i * ROWS
        receiver = jnp.where(edge < live, grecv[:, at(i)], -1)
        total[...] += dot(scatter(receiver, nodes), message)

    loop(gfeat.shape[0] // ROWS, enc_edges)

    def mesh_step(current, weights, first):
        before = dot(current, weights[first]) + dot(total[...].astype(BF), weights[first + 1])
        hidden = silu(before).astype(BF)
        return (current.astype(F32) + layer_norm(dot(hidden, weights[first + 2]))).astype(BF)

    mnext[...] = mesh_step(mesh[...], encw, 4)

    need("p01")
    pown[...] = dot(mnext[...], procw[0]).astype(BF)
    pcoarse[patch, band] = pown[nodes - COARSE_DEV :]
    p_north, p_south, p_flat, p_north_on, p_south_on = near_copies(pown, pnear, P_SIDE, P_FORWARD)
    start_sides(p_north, p_south, p_flat)
    columns = []
    for k in range(1, bands):
        own = pcoarse.at[patch, band]
        there = pcoarse.at[patch, lax.rem(band + bands - k, bands)]
        columns.append(
            (
                remote(own, own, C_BASE + k, lax.rem(band + k, bands), patch),
                remote(there, there, C_BASE + k, lax.rem(band + k, bands), patch),
            )
        )
    for out_copy, _ in columns:
        out_copy.start()
    precv_rows[...] = dot(mnext[...], procw[1]).astype(BF)
    need("ps", "pr")

    shift = patches.bit_length() - 1

    def node_place(s):
        q = s >> 8
        slot = jnp.where(q > 4, q - 1, q)
        near = jnp.where(q == 4, s - 4 * nodes, nodes + slot * BORDER + (s & (nodes - 1)))
        c = s - 9 * nodes
        device = c >> 4
        distant = ((device & (patches - 1)) * bands + (device >> shift)) * COARSE_DEV + (c & (COARSE_DEV - 1))
        return jnp.where(c < 0, near, distant + nodes + 8 * BORDER)

    def proc_own(i):
        place = columns_of(node_place(psend[:, at(i)]))
        recv = columns_of(precv[:, at(i)])
        left = jnp.concatenate([pick(place, 0, nodes), pick(recv, 0, nodes)], axis=1)
        right = jnp.concatenate([pown[...], precv_rows[...]], axis=0)
        pre_p[at(i)] = pre_p[at(i)] + dot(left, right)

    pass_on(p_north, p_south, p_north_on, p_south_on)
    for _, in_copy in columns:
        in_copy.wait_recv()
    cores = 2
    count = patches // cores
    base = C_BASE + bands
    mate = patch + 1 - 2 * lax.rem(patch, 2)
    across, over = [], []
    for k in range(count):
        column = lax.rem(patch + patches - cores * k, patches)
        mate_column = lax.rem(mate + patches - cores * k, patches)
        src, got = pcoarse.at[column], pcoarse.at[mate_column]
        over.append(
            (remote(src, src, base + count + k, band, mate), remote(got, got, base + count + k, band, mate))
        )
        if k:
            to = lax.rem(patch + cores * k, patches)
            own = pcoarse.at[patch]
            across.append((remote(own, own, base + k, band, to), remote(src, src, base + k, band, to)))
    for out_copy, _ in across:
        out_copy.start()
    over[0][0].start()
    loop(pfeat.shape[0] // ROWS, proc_own)
    for k, (_, in_copy) in enumerate(across):
        in_copy.wait_recv()
        over[k + 1][0].start()

    def dec_update(i):
        upd[at(i)] = dot(gnext[at(i)], decw[4])

    loop(grid_steps, dec_update)
    for _, in_copy in over:
        in_copy.wait_recv()
    for out_copy, _ in columns + across + over:
        out_copy.wait_send()
    finish(p_north, p_south, p_flat, p_north_on, p_south_on)

    need("p36")
    total[...] = jnp.zeros_like(total)
    far = 8 * BORDER + bands * patches * COARSE_DEV

    def proc_edges(i):
        place = columns_of(node_place(psend[:, at(i)]))
        right = jnp.concatenate(
            [pnear[...].reshape(8 * BORDER, latent), pcoarse[...].reshape(far - 8 * BORDER, latent)], axis=0
        )
        before = pre_p[at(i)] + dot(pick(place, nodes, far), right)
        message = layer_norm(dot(silu(before).astype(BF), procw[3])).astype(BF)
        total[...] += dot(scatter(precv[:, at(i)], nodes), message)

    loop(pfeat.shape[0] // ROWS, proc_edges)
    last = mesh_step(mnext[...], procw, 4)

    down[...] = dot(last, decw[0]).astype(BF)
    d_north, d_south, d_flat, d_north_on, d_south_on = near_copies(down, dnear, D_SIDE, D_FORWARD)
    start_sides(d_north, d_south, d_flat)

    def dec_columns(k, i):
        rows = [dsend[k, pl.ds(i * half_lat + r, 1), :] for r in range(half_lat)]
        return columns_of(node_place(jnp.concatenate(rows, axis=1)))

    def dec_own(i):
        for k in range(3):
            pre_d[k, at(i)] = pre_d[k, at(i)] + dot(pick(dec_columns(k, i), 0, nodes), down[...])

    dec_own(0)
    pass_on(d_north, d_south, d_north_on, d_south_on)
    dec_own(1)
    finish(d_north, d_south, d_flat, d_north_on, d_south_on)

    def dec_edges(i):
        near = dnear[...].reshape(8 * BORDER, latent)
        summed = jnp.zeros((ROWS, latent), F32)
        for k in range(3):
            before = pre_d[k, at(i)] + dot(pick(dec_columns(k, i), nodes, 8 * BORDER), near)
            message = layer_norm(dot(silu(before).astype(BF), decw[3])).astype(BF)
            summed = summed + message.astype(F32)
        hidden = silu(upd[at(i)] + dot(summed.astype(BF), decw[5])).astype(BF)
        rows = (gnext[at(i)].astype(F32) + layer_norm(dot(hidden, decw[6]))).astype(BF)
        result[pl.ds(i * half_lat, half_lat)] = rows.reshape(half_lat, lon, latent)

    stores = []
    for i in range(grid_steps):
        dec_edges(i)
        part = pl.ds(i * half_lat, half_lat)
        stores.append(pltpu.make_async_copy(result.at[part], out.at[part], out_sem.at[i]))
        stores[-1].start()
    for copy in stores:
        copy.wait()


def solution(mesh):
    bands, patches = mesh.shape["band"], mesh.shape["patch"]

    def shards(grid, mesh_state, gfeat, gsend, grecv, blocks, pfeat, psend, precv, dfeat, dsend, encw, procw, decw):
        lat, lon, latent = grid.shape
        nodes = mesh_state.shape[2]
        edges, pedges = gfeat.shape[2], pfeat.shape[2]
        cells = lat * lon
        any_spec = pl.BlockSpec(memory_space=pl.ANY)
        vmem = pltpu.VMEM
        copies = C_BASE + bands + patches
        return pl.pallas_call(
            functools.partial(body, bands, patches),
            out_shape=jax.ShapeDtypeStruct(grid.shape, BF),
            in_specs=[any_spec] * 5 + [pl.BlockSpec(memory_space=pltpu.SMEM)] + [any_spec] * 8,
            out_specs=any_spec,
            scratch_shapes=[
                vmem(grid.shape, BF),
                vmem((nodes, latent), BF),
                vmem((edges, latent), BF),
                vmem((1, edges), jnp.int32),
                vmem((1, edges), jnp.int32),
                vmem((pedges, latent), BF),
                vmem((1, pedges), jnp.int32),
                vmem((1, pedges), jnp.int32),
                vmem(dfeat.shape, BF),
                vmem(dsend.shape, jnp.int32),
                vmem(encw.shape, BF),
                vmem(procw.shape, BF),
                vmem(decw.shape, BF),
                vmem((9, lon // 16, 16, latent), BF),
                vmem((nodes, latent), BF),
                vmem((cells, latent), BF),
                vmem((edges, latent), F32),
                vmem((pedges, latent), F32),
                vmem((3, cells, latent), F32),
                vmem((cells, latent), F32),
                vmem((nodes, latent), F32),
                vmem((nodes, latent), BF),
                vmem((nodes, latent), BF),
                vmem((8, BORDER, latent), BF),
                vmem((patches, bands, COARSE_DEV, latent), BF),
                vmem((nodes, latent), BF),
                vmem((nodes, latent), BF),
                vmem((8, BORDER, latent), BF),
                vmem(grid.shape, BF),
                pltpu.SemaphoreType.DMA((18,)),
                pltpu.SemaphoreType.DMA((2,)),
                pltpu.SemaphoreType.DMA((copies,)),
                pltpu.SemaphoreType.DMA((copies,)),
            ],
            compiler_params=pltpu.CompilerParams(
                collective_id=0, has_side_effects=True, vmem_limit_bytes=62 * 1024 * 1024
            ),
            cost_estimate=pl.CostEstimate(flops=24 * 10**9, bytes_accessed=24 * 10**6, transcendentals=5 * 10**6),
        )(grid, mesh_state, gfeat, gsend, grecv, blocks, pfeat, psend, precv, dfeat, dsend, encw, procw, decw)

    placed = (
        P("band", "patch", None),
        P("band", "patch", None, None),
        P("band", "patch", None, None),
        P("band", "patch", None),
        P("band", "patch", None),
        P(),
        P("band", "patch", None, None),
        P("band", "patch", None),
        P("band", "patch", None),
        P(None, "band", "patch", None),
        P(None, "band", "patch"),
        P(),
        P(),
        P(),
    )
    return jax.shard_map(
        shards, mesh=mesh, in_specs=placed, out_specs=P("band", "patch", None), check_vma=False
    )
```

```python
import functools

import jax
import jax.numpy as jnp
from jax import lax
from jax.experimental import pallas as pl
from jax.experimental.pallas import tpu as pltpu
from jax.sharding import PartitionSpec as P

MESH = pl.DeviceIdType.MESH
COARSE_DEV = 16
HALO = 2
BORDER = 64
EPSILON = 1e-05
BF = jnp.bfloat16
F32 = jnp.float32
ROWS = 512

G_NORTH, G_SOUTH, G_WEST, G_EAST = 0, 3, 6, 7
G_FORWARD = 8
P_FIRST, D_FIRST = 12, 26
C_BASE = 40


def dot(a, b):
    return jnp.dot(a, b, preferred_element_type=F32)


def silu(v):
    half = 0.5 * v
    return half + half * jnp.tanh(half)


def layer_norm(v):
    centred = v - jnp.mean(v, axis=-1, keepdims=True)
    spread = jnp.mean(centred * centred, axis=-1, keepdims=True)
    return centred * lax.rsqrt(spread + EPSILON)


def columns_of(row):
    n = row.shape[1]
    wide = jnp.broadcast_to(row.astype(F32), (128, n)).T
    return wide.astype(jnp.int32).astype(jnp.int16)


def pick(columns, first, count):
    lane = lax.broadcasted_iota(jnp.int16, columns.shape, 1)
    parts = []
    for start in range(first, first + count, 128):
        hit = columns == lane + jnp.int16(start)
        parts.append(jnp.where(hit, BF(1), BF(0)))
    return jnp.concatenate(parts, axis=1) if len(parts) > 1 else parts[0]


def scatter(row, nodes):
    hit = lax.broadcasted_iota(jnp.int32, (nodes, row.shape[1]), 0) == row
    return jnp.where(hit, 1.0, 0.0).astype(BF)


def body(
    bands,
    patches,
    grid_in,
    mesh_in,
    gfeat_in,
    gsend_in,
    grecv_in,
    blocks_in,
    pfeat_in,
    psend_in,
    precv_in,
    dfeat_in,
    dsend_in,
    encw_in,
    procw_in,
    decw_in,
    out,
    grid,
    mesh,
    gfeat,
    gsend,
    grecv,
    pfeat,
    psend,
    precv,
    dfeat,
    dsend,
    encw,
    procw,
    decw,
    table,
    mrecv,
    gnext,
    pre_e,
    pre_d,
    upd,
    base,
    cols_g,
    cols_p,
    cols_d,
    blocks,
    total,
    mnext,
    pown,
    pnear,
    pcoarse,
    precv_rows,
    recv_d,
    down,
    dnear,
    result,
    in_sem,
    out_sem,
    send_sem,
    recv_sem,
):
    band, patch = lax.axis_index("band"), lax.axis_index("patch")
    has_north, has_south = band > 0, band < bands - 1
    west, east = lax.rem(patch + patches - 1, patches), lax.rem(patch + 1, patches)
    lat, lon, latent = grid.shape
    nodes = mesh.shape[0]
    half_lat = ROWS // lon

    loads = {}

    def load(name, src, dst):
        copy = pltpu.make_async_copy(src, dst, in_sem.at[len(loads)])
        copy.start()
        loads[name] = copy

    load("e0", encw_in.at[0], encw.at[0])
    load("grid", grid_in, grid)
    load("e78", encw_in.at[pl.ds(7, 2)], encw.at[pl.ds(7, 2)])
    load("mesh", mesh_in.at[0, 0], mesh)
    load("e12", encw_in.at[pl.ds(1, 2)], encw.at[pl.ds(1, 2)])
    load("gs", gsend_in.at[0], gsend)
    load("gr", grecv_in.at[0], grecv)
    load("ps", psend_in.at[0], psend)
    load("pr", precv_in.at[0], precv)
    load("ds", dsend_in, dsend)
    load("blocks", blocks_in, blocks)
    load("gf", gfeat_in.at[0, 0], gfeat)
    load("p2", procw_in.at[2], procw.at[2])
    load("pf", pfeat_in.at[0, 0], pfeat)
    load("e36", encw_in.at[pl.ds(3, 4)], encw.at[pl.ds(3, 4)])
    load("p01", procw_in.at[pl.ds(0, 2)], procw.at[pl.ds(0, 2)])
    load("d", decw_in, decw)
    load("df", dfeat_in, dfeat)
    load("p36", procw_in.at[pl.ds(3, 4)], procw.at[pl.ds(3, 4)])

    def need(*names):
        for name in names:
            loads[name].wait()

    barrier = pltpu.get_barrier_semaphore()
    for k in range(1, bands):
        pl.semaphore_signal(
            barrier, inc=1, device_id={"band": lax.rem(band + k, bands), "patch": patch}, device_id_type=MESH
        )
    greeted = [k for k in range(1, patches) if k in (1, patches - 1) or k % 2 == 0]
    for k in greeted:
        pl.semaphore_signal(
            barrier, inc=1, device_id={"band": band, "patch": lax.rem(patch + k, patches)}, device_id_type=MESH
        )

    def remote(src, dst, number, to_band, to_patch):
        return pltpu.make_async_remote_copy(
            src_ref=src,
            dst_ref=dst,
            send_sem=send_sem.at[number],
            recv_sem=recv_sem.at[number],
            device_id={"band": to_band, "patch": to_patch},
            device_id_type=MESH,
        )

    @pl.when(jnp.logical_not(has_north))
    def _():
        table[4:6] = jnp.zeros_like(table[4:6])
        table[8, 8:12] = jnp.zeros_like(table[8, 8:12])
        pnear[0:3] = jnp.zeros_like(pnear[0:3])
        dnear[0:3] = jnp.zeros_like(dnear[0:3])

    @pl.when(jnp.logical_not(has_south))
    def _():
        table[6:8] = jnp.zeros_like(table[6:8])
        table[8, 12:16] = jnp.zeros_like(table[8, 12:16])
        pnear[5:8] = jnp.zeros_like(pnear[5:8])
        dnear[5:8] = jnp.zeros_like(dnear[5:8])

    groups = lon // 16
    north_band, south_band = lax.rem(band + bands - 1, bands), lax.rem(band + 1, bands)
    cuts = ((0, 1), (groups - 1, 1), (1, groups - 2))
    g_north = [
        remote(
            table.at[pl.ds(0, 2), pl.ds(a, n)], table.at[pl.ds(6, 2), pl.ds(a, n)], G_NORTH + i, north_band, patch
        )
        for i, (a, n) in enumerate(cuts)
    ]
    g_south = [
        remote(
            table.at[pl.ds(2, 2), pl.ds(a, n)], table.at[pl.ds(4, 2), pl.ds(a, n)], G_SOUTH + i, south_band, patch
        )
        for i, (a, n) in enumerate(cuts)
    ]
    g_west = remote(table.at[pl.ds(0, 4), 0], table.at[8, pl.ds(4, 4)], G_WEST, band, west)
    g_east = remote(table.at[pl.ds(0, 4), groups - 1], table.at[8, pl.ds(0, 4)], G_EAST, band, east)
    g_north_on = [
        remote(table.at[pl.ds(4, 2), 0], table.at[8, pl.ds(10, 2)], G_FORWARD, band, west),
        remote(table.at[pl.ds(4, 2), groups - 1], table.at[8, pl.ds(8, 2)], G_FORWARD + 1, band, east),
    ]
    g_south_on = [
        remote(table.at[pl.ds(6, 2), 0], table.at[8, pl.ds(14, 2)], G_FORWARD + 2, band, west),
        remote(table.at[pl.ds(6, 2), groups - 1], table.at[8, pl.ds(12, 2)], G_FORWARD + 3, band, east),
    ]

    chunk = BORDER // 2

    def near_copies(own, near, first):
        rows = own.at[pl.ds(0, BORDER)]
        flat = [remote(rows, near.at[4], first, band, west), remote(rows, near.at[3], first + 1, band, east)]
        norths, souths, norths_on, souths_on = [], [], [], []
        for c in range(2):
            n = first + 2 + 6 * c
            part = pl.ds(c * chunk, chunk)
            norths.append(remote(own.at[part], near.at[6, part], n, north_band, patch))
            souths.append(remote(own.at[part], near.at[1, part], n + 1, south_band, patch))
            norths_on += [
                remote(near.at[1, part], near.at[2, part], n + 2, band, west),
                remote(near.at[1, part], near.at[0, part], n + 3, band, east),
            ]
            souths_on += [
                remote(near.at[6, part], near.at[7, part], n + 4, band, west),
                remote(near.at[6, part], near.at[5, part], n + 5, band, east),
            ]
        return norths, souths, flat, norths_on, souths_on

    def pass_chunk(c, norths, souths, flat, norths_on, souths_on):
        two = slice(2 * c, 2 * c + 2)
        pass_on(norths[c : c + 1], souths[c : c + 1], norths_on[two], souths_on[two])

    def when_all(condition, copies, method):
        @pl.when(condition)
        def _():
            for copy in copies:
                getattr(copy, method)()

    def start_sides(north, south, flat):
        when_all(has_north, north, "start")
        when_all(has_south, south, "start")
        for copy in flat:
            copy.start()

    def pass_on(from_south, from_north, north_on, south_on):
        when_all(has_north, from_north, "wait_recv")
        when_all(has_north, north_on, "start")
        when_all(has_south, from_south, "wait_recv")
        when_all(has_south, south_on, "start")

    def finish(north, south, flat, north_on, south_on):
        for copy in flat:
            copy.wait_recv()
        when_all(has_north, north_on, "wait_recv")
        when_all(has_south, south_on, "wait_recv")
        when_all(has_north, north, "wait_send")
        when_all(has_south, south, "wait_send")
        for copy in flat:
            copy.wait_send()
        when_all(has_north, north_on, "wait_send")
        when_all(has_south, south_on, "wait_send")

    def loop(count, step, unroll=1):
        def one(i, carry):
            step(i)
            return carry

        lax.fori_loop(0, count, one, 0, unroll=unroll)

    def at(i):
        return pl.ds(pl.multiple_of(i * ROWS, ROWS), ROWS)

    grid_steps = lat * lon // ROWS

    def grid_rows(i):
        return grid[pl.ds(i * half_lat, half_lat)].reshape(ROWS, latent)

    need("grid", "e0")

    def send_step(i):
        rows = dot(grid_rows(i), encw[0]).astype(BF)
        table[pl.ds(i * half_lat, half_lat)] = rows.reshape(half_lat, groups, 16, latent)

    send_step(0)
    pl.semaphore_wait(barrier, bands - 1 + len(greeted))
    when_all(has_north, g_north, "start")
    for i in range(1, grid_steps):
        send_step(i)
    when_all(has_south, g_south, "start")
    g_west.start()
    g_east.start()

    need("e78")

    def self_step(i):
        rows = grid_rows(i)
        hidden = silu(dot(rows, encw[7])).astype(BF)
        gnext[at(i)] = (rows.astype(F32) + layer_norm(dot(hidden, encw[8]))).astype(BF)

    loop(grid_steps, self_step)
    need("mesh", "e12")
    mrecv[...] = dot(mesh[...], encw[1]).astype(BF)
    need("e36")
    base[...] = dot(mesh[...], encw[4])
    pass_on(g_north[:2], g_south[:2], g_north_on, g_south_on)

    width = lon + 2 * HALO

    def grid_place(s):
        i = jnp.zeros_like(s)
        for k in range(1, lat + 2 * HALO):
            i = i + (s >= k * width).astype(jnp.int32)
        j = s - i * width
        north, south = i < HALO, i >= lat + HALO
        line = jnp.where(north, i + 4, jnp.where(south, i, i - 2))
        inner = line * lon + j - HALO
        left = jnp.where(north, i + 8, jnp.where(south, i + 6, i - 2)) * 16 + j + 14
        right = jnp.where(north, i + 10, jnp.where(south, i + 8, i + 2)) * 16 + j - (lon + HALO)
        edge = 8 * lon + jnp.where(j < HALO, left, right)
        return jnp.where((j < HALO) | (j >= lon + HALO), edge, inner)

    shift = patches.bit_length() - 1

    def node_place(s):
        q = s >> 8
        slot = jnp.where(q > 4, q - 1, q)
        near = jnp.where(q == 4, s - 4 * nodes, nodes + slot * BORDER + (s & (nodes - 1)))
        c = s - 9 * nodes
        device = c >> 4
        distant = ((device & (patches - 1)) * bands + (device >> shift)) * COARSE_DEV + (c & (COARSE_DEV - 1))
        return jnp.where(c < 0, near, distant + nodes + 8 * BORDER)

    def dec_columns(k, i):
        rows = [dsend[k, pl.ds(i * half_lat + r, 1), :] for r in range(half_lat)]
        return columns_of(node_place(jnp.concatenate(rows, axis=1)))

    need("gs", "gr", "gf")

    def enc_own(i):
        place = columns_of(grid_place(gsend[:, at(i)]))
        cols_g[at(i)] = place
        recv = columns_of(grecv[:, at(i)])
        left = jnp.concatenate([gfeat[at(i)], pick(place, 0, 4 * lon), pick(recv, 0, nodes)], axis=1)
        right = jnp.concatenate([encw[2], table[0:4].reshape(4 * lon, latent), mrecv[...]], axis=0)
        pre_e[at(i)] = dot(left, right)

    loop(gfeat.shape[0] // ROWS, enc_own)
    need("ps", "pr", "ds")

    def proc_place(i):
        cols_p[at(i)] = columns_of(node_place(psend[:, at(i)]))

    loop(pfeat.shape[0] // ROWS, proc_place)

    def dec_place(i):
        for k in range(3):
            cols_d[k, at(i)] = dec_columns(k, i)

    loop(grid_steps, dec_place)
    need("d")

    def dec_grid(i):
        recv_d[at(i)] = dot(gnext[at(i)], decw[1]).astype(BF)

    loop(grid_steps, dec_grid)
    need("blocks", "p2", "pf", "p01", "df")

    when_all(has_south, g_north[2:], "wait_recv")
    when_all(has_north, g_south[2:], "wait_recv")
    finish(g_north, g_south, [g_west, g_east], g_north_on, g_south_on)
    total[...] = jnp.zeros_like(total)
    live = blocks[band, patch] * 128

    def enc_edges(i):
        before = pre_e[at(i)] + dot(pick(cols_g[at(i)], 4 * lon, 5 * lon), table[4:9].reshape(5 * lon, latent))
        message = layer_norm(dot(silu(before).astype(BF), encw[3])).astype(BF)
        edge = lax.broadcasted_iota(jnp.int32, (1, ROWS), 1) + i * ROWS
        receiver = jnp.where(edge < live, grecv[:, at(i)], -1)
        total[...] += dot(scatter(receiver, nodes), message)

    loop(gfeat.shape[0] // ROWS, enc_edges, 2)

    def mesh_step(current, weights, first):
        before = base[...] + dot(total[...].astype(BF), weights[first + 1])
        hidden = silu(before).astype(BF)
        return (current.astype(F32) + layer_norm(dot(hidden, weights[first + 2]))).astype(BF)

    mnext[...] = mesh_step(mesh[...], encw, 4)

    pown[...] = dot(mnext[...], procw[0]).astype(BF)
    pcoarse[patch, band] = pown[nodes - COARSE_DEV :]
    p_near = near_copies(pown, pnear, P_FIRST)
    columns = []
    for k in range(1, bands):
        own = pcoarse.at[patch, band]
        there = pcoarse.at[patch, lax.rem(band + bands - k, bands)]
        columns.append(
            (
                remote(own, own, C_BASE + k, lax.rem(band + k, bands), patch),
                remote(there, there, C_BASE + k, lax.rem(band + k, bands), patch),
            )
        )
    for out_copy, _ in columns:
        out_copy.start()
    start_sides(*p_near[:3])
    precv_rows[...] = dot(mnext[...], procw[1]).astype(BF)
    need("p36")
    base[...] = dot(mnext[...], procw[4])

    def proc_own(i):
        recv = columns_of(precv[:, at(i)])
        left = jnp.concatenate([pfeat[at(i)], pick(cols_p[at(i)], 0, nodes), pick(recv, 0, nodes)], axis=1)
        right = jnp.concatenate([procw[2], pown[...], precv_rows[...]], axis=0)
        pre_e[at(i)] = dot(left, right)

    def dec_update(i):
        upd[at(i)] = dot(gnext[at(i)], decw[4])

    loop(grid_steps, dec_update)

    for _, in_copy in columns:
        in_copy.wait_recv()
    cores = 2
    count = patches // cores
    first_id = C_BASE + bands
    mate = patch + 1 - 2 * lax.rem(patch, 2)
    across, over = [], []
    for k in range(count):
        column = lax.rem(patch + patches - cores * k, patches)
        mate_column = lax.rem(mate + patches - cores * k, patches)
        src, got = pcoarse.at[column], pcoarse.at[mate_column]
        over.append(
            (remote(src, src, first_id + count + k, band, mate), remote(got, got, first_id + count + k, band, mate))
        )
        if k:
            to = lax.rem(patch + cores * k, patches)
            own = pcoarse.at[patch]
            across.append((remote(own, own, first_id + k, band, to), remote(src, src, first_id + k, band, to)))
    for out_copy, _ in across:
        out_copy.start()
    over[0][0].start()
    pass_chunk(0, *p_near)
    half = pfeat.shape[0] // ROWS // 2
    loop(half, proc_own)
    pass_chunk(1, *p_near)
    for k, (_, in_copy) in enumerate(across):
        in_copy.wait_recv()
        over[k + 1][0].start()

    loop(pfeat.shape[0] // ROWS - half, lambda i: proc_own(i + half))
    for _, in_copy in over:
        in_copy.wait_recv()
    for out_copy, _ in columns + across + over:
        out_copy.wait_send()
    finish(*p_near)

    total[...] = jnp.zeros_like(total)
    far = 8 * BORDER + bands * patches * COARSE_DEV

    def proc_edges(i):
        right = jnp.concatenate(
            [pnear[...].reshape(8 * BORDER, latent), pcoarse[...].reshape(far - 8 * BORDER, latent)], axis=0
        )
        before = pre_e[at(i)] + dot(pick(cols_p[at(i)], nodes, far), right)
        message = layer_norm(dot(silu(before).astype(BF), procw[3])).astype(BF)
        total[...] += dot(scatter(precv[:, at(i)], nodes), message)

    loop(pfeat.shape[0] // ROWS, proc_edges, 2)
    last = mesh_step(mnext[...], procw, 4)

    down[...] = dot(last, decw[0]).astype(BF)
    d_near = near_copies(down, dnear, D_FIRST)
    start_sides(*d_near[:3])

    def dec_own(i):
        recv = recv_d[at(i)].astype(F32)
        right = jnp.concatenate([decw[2], down[...]], axis=0)
        for k in range(3):
            rows = dfeat[k, pl.ds(i * half_lat, half_lat)].reshape(ROWS, latent)
            left = jnp.concatenate([rows, pick(cols_d[k, at(i)], 0, nodes)], axis=1)
            pre_d[k, at(i)] = dot(left, right) + recv

    dec_own(0)
    pass_chunk(0, *d_near)
    for i in range(1, grid_steps):
        dec_own(i)
    pass_chunk(1, *d_near)
    finish(*d_near)

    def dec_edges(i):
        near = dnear[...].reshape(8 * BORDER, latent)
        summed = jnp.zeros((ROWS, latent), F32)
        for k in range(3):
            before = pre_d[k, at(i)] + dot(pick(cols_d[k, at(i)], nodes, 8 * BORDER), near)
            message = layer_norm(dot(silu(before).astype(BF), decw[3])).astype(BF)
            summed = summed + message.astype(F32)
        hidden = silu(upd[at(i)] + dot(summed.astype(BF), decw[5])).astype(BF)
        rows = (gnext[at(i)].astype(F32) + layer_norm(dot(hidden, decw[6]))).astype(BF)
        result[pl.ds(i * half_lat, half_lat)] = rows.reshape(half_lat, lon, latent)

    stores = []
    for i in range(grid_steps):
        dec_edges(i)
        part = pl.ds(i * half_lat, half_lat)
        stores.append(pltpu.make_async_copy(result.at[part], out.at[part], out_sem.at[i]))
        stores[-1].start()
    for copy in stores:
        copy.wait()


def solution(mesh):
    bands, patches = mesh.shape["band"], mesh.shape["patch"]

    def shards(grid, mesh_state, gfeat, gsend, grecv, blocks, pfeat, psend, precv, dfeat, dsend, encw, procw, decw):
        lat, lon, latent = grid.shape
        nodes = mesh_state.shape[2]
        edges, pedges = gfeat.shape[2], pfeat.shape[2]
        cells = lat * lon
        any_spec = pl.BlockSpec(memory_space=pl.ANY)
        vmem = pltpu.VMEM
        copies = C_BASE + bands + patches
        return pl.pallas_call(
            functools.partial(body, bands, patches),
            out_shape=jax.ShapeDtypeStruct(grid.shape, BF),
            in_specs=[any_spec] * 14,
            out_specs=any_spec,
            scratch_shapes=[
                vmem(grid.shape, BF),
                vmem((nodes, latent), BF),
                vmem((edges, latent), BF),
                vmem((1, edges), jnp.int32),
                vmem((1, edges), jnp.int32),
                vmem((pedges, latent), BF),
                vmem((1, pedges), jnp.int32),
                vmem((1, pedges), jnp.int32),
                vmem(dfeat.shape, BF),
                vmem(dsend.shape, jnp.int32),
                vmem(encw.shape, BF),
                vmem(procw.shape, BF),
                vmem(decw.shape, BF),
                vmem((9, lon // 16, 16, latent), BF),
                vmem((nodes, latent), BF),
                vmem((cells, latent), BF),
                vmem((max(edges, pedges), latent), F32),
                vmem((3, cells, latent), F32),
                vmem((cells, latent), F32),
                vmem((nodes, latent), F32),
                vmem((edges, 128), jnp.int16),
                vmem((pedges, 128), jnp.int16),
                vmem((3, cells, 128), jnp.int16),
                pltpu.SMEM((bands, patches), jnp.int32),
                vmem((nodes, latent), F32),
                vmem((nodes, latent), BF),
                vmem((nodes, latent), BF),
                vmem((8, BORDER, latent), BF),
                vmem((patches, bands, COARSE_DEV, latent), BF),
                vmem((nodes, latent), BF),
                vmem((cells, latent), BF),
                vmem((nodes, latent), BF),
                vmem((8, BORDER, latent), BF),
                vmem(grid.shape, BF),
                pltpu.SemaphoreType.DMA((19,)),
                pltpu.SemaphoreType.DMA((2,)),
                pltpu.SemaphoreType.DMA((copies,)),
                pltpu.SemaphoreType.DMA((copies,)),
            ],
            compiler_params=pltpu.CompilerParams(
                collective_id=0, has_side_effects=True, vmem_limit_bytes=62 * 1024 * 1024
            ),
            cost_estimate=pl.CostEstimate(flops=24 * 10**9, bytes_accessed=24 * 10**6, transcendentals=5 * 10**6),
        )(grid, mesh_state, gfeat, gsend, grecv, blocks, pfeat, psend, precv, dfeat, dsend, encw, procw, decw)

    placed = (
        P("band", "patch", None),
        P("band", "patch", None, None),
        P("band", "patch", None, None),
        P("band", "patch", None),
        P("band", "patch", None),
        P(),
        P("band", "patch", None, None),
        P("band", "patch", None),
        P("band", "patch", None),
        P(None, "band", "patch", None),
        P(None, "band", "patch"),
        P(),
        P(),
        P(),
    )
    return jax.shard_map(
        shards, mesh=mesh, in_specs=placed, out_specs=P("band", "patch", None), check_vma=False
    )
```

```python
import functools

import jax
import jax.numpy as jnp
from jax import lax
from jax.experimental import pallas as pl
from jax.experimental.pallas import tpu as pltpu
from jax.sharding import PartitionSpec as P

MESH = pl.DeviceIdType.MESH
COARSE_DEV = 16
HALO = 2
BORDER = 64
EPSILON = 1e-05
BF = jnp.bfloat16
F32 = jnp.float32
ROWS = 512

G_NORTH, G_SOUTH, G_WEST, G_EAST = 0, 4, 8, 9
G_FORWARD = 10
P_FIRST, D_FIRST = 14, 28
C_BASE = 42


def dot(a, b):
    return jnp.dot(a, b, preferred_element_type=F32)


def silu(v):
    half = 0.5 * v
    return half + half * jnp.tanh(half)


def layer_norm(v):
    centred = v - jnp.mean(v, axis=-1, keepdims=True)
    spread = jnp.mean(centred * centred, axis=-1, keepdims=True)
    return centred * lax.rsqrt(spread + EPSILON)


def columns_of(row):
    n = row.shape[1]
    wide = jnp.broadcast_to(row.astype(F32), (128, n)).T
    return wide.astype(jnp.int32).astype(jnp.int16)


def pick(columns, first, count):
    lane = lax.broadcasted_iota(jnp.int16, columns.shape, 1)
    parts = []
    for start in range(first, first + count, 128):
        hit = columns == lane + jnp.int16(start)
        parts.append(jnp.where(hit, BF(1), BF(0)))
    return jnp.concatenate(parts, axis=1) if len(parts) > 1 else parts[0]


def scatter(row, nodes):
    hit = lax.broadcasted_iota(jnp.int32, (nodes, row.shape[1]), 0) == row
    return jnp.where(hit, 1.0, 0.0).astype(BF)


def body(
    bands,
    patches,
    grid_in,
    mesh_in,
    gfeat_in,
    gsend_in,
    grecv_in,
    blocks_in,
    pfeat_in,
    psend_in,
    precv_in,
    dfeat_in,
    dsend_in,
    encw_in,
    procw_in,
    decw_in,
    out,
    grid,
    mesh,
    gfeat,
    gsend,
    grecv,
    pfeat,
    psend,
    precv,
    dfeat,
    dsend,
    encw,
    procw,
    decw,
    table,
    mrecv,
    gnext,
    pre_e,
    pre_d,
    upd,
    base,
    cols_g,
    cols_p,
    cols_d,
    blocks,
    total,
    mnext,
    pown,
    pnear,
    pcoarse,
    precv_rows,
    recv_d,
    down,
    dnear,
    result,
    in_sem,
    out_sem,
    send_sem,
    recv_sem,
):
    band, patch = lax.axis_index("band"), lax.axis_index("patch")
    has_north, has_south = band > 0, band < bands - 1
    west, east = lax.rem(patch + patches - 1, patches), lax.rem(patch + 1, patches)
    lat, lon, latent = grid.shape
    nodes = mesh.shape[0]
    half_lat = ROWS // lon

    loads = {}

    def load(name, src, dst):
        copy = pltpu.make_async_copy(src, dst, in_sem.at[len(loads)])
        copy.start()
        loads[name] = copy

    load("e0", encw_in.at[0], encw.at[0])
    load("grid", grid_in, grid)
    load("e78", encw_in.at[pl.ds(7, 2)], encw.at[pl.ds(7, 2)])
    load("mesh", mesh_in.at[0, 0], mesh)
    load("e12", encw_in.at[pl.ds(1, 2)], encw.at[pl.ds(1, 2)])
    load("gs", gsend_in.at[0], gsend)
    load("gr", grecv_in.at[0], grecv)
    load("ps", psend_in.at[0], psend)
    load("pr", precv_in.at[0], precv)
    load("ds", dsend_in, dsend)
    load("blocks", blocks_in, blocks)
    load("gf", gfeat_in.at[0, 0], gfeat)
    load("p2", procw_in.at[2], procw.at[2])
    load("pf", pfeat_in.at[0, 0], pfeat)
    load("e36", encw_in.at[pl.ds(3, 4)], encw.at[pl.ds(3, 4)])
    load("p01", procw_in.at[pl.ds(0, 2)], procw.at[pl.ds(0, 2)])
    load("d", decw_in, decw)
    load("df", dfeat_in, dfeat)
    load("p36", procw_in.at[pl.ds(3, 4)], procw.at[pl.ds(3, 4)])

    def need(*names):
        for name in names:
            loads[name].wait()

    barrier = pltpu.get_barrier_semaphore()
    for k in range(1, bands):
        pl.semaphore_signal(
            barrier, inc=1, device_id={"band": lax.rem(band + k, bands), "patch": patch}, device_id_type=MESH
        )
    greeted = [k for k in range(1, patches) if k in (1, patches - 1) or k % 2 == 0]
    for k in greeted:
        pl.semaphore_signal(
            barrier, inc=1, device_id={"band": band, "patch": lax.rem(patch + k, patches)}, device_id_type=MESH
        )

    def remote(src, dst, number, to_band, to_patch):
        return pltpu.make_async_remote_copy(
            src_ref=src,
            dst_ref=dst,
            send_sem=send_sem.at[number],
            recv_sem=recv_sem.at[number],
            device_id={"band": to_band, "patch": to_patch},
            device_id_type=MESH,
        )

    @pl.when(jnp.logical_not(has_north))
    def _():
        table[4:6] = jnp.zeros_like(table[4:6])
        table[8, 8:12] = jnp.zeros_like(table[8, 8:12])
        pnear[0] = jnp.zeros_like(pnear[0])
        pnear[4:6] = jnp.zeros_like(pnear[4:6])
        dnear[0] = jnp.zeros_like(dnear[0])
        dnear[4:6] = jnp.zeros_like(dnear[4:6])

    @pl.when(jnp.logical_not(has_south))
    def _():
        table[6:8] = jnp.zeros_like(table[6:8])
        table[8, 12:16] = jnp.zeros_like(table[8, 12:16])
        pnear[1] = jnp.zeros_like(pnear[1])
        pnear[6:8] = jnp.zeros_like(pnear[6:8])
        dnear[1] = jnp.zeros_like(dnear[1])
        dnear[6:8] = jnp.zeros_like(dnear[6:8])

    groups = lon // 16
    north_band, south_band = lax.rem(band + bands - 1, bands), lax.rem(band + 1, bands)
    cuts = ((0, 2, 0, 1), (0, 2, groups - 1, 1), (0, 1, 1, groups - 2), (1, 1, 1, groups - 2))

    def halo(start, landing, first, to_band):
        return [
            remote(
                table.at[pl.ds(start + r, rows), pl.ds(g, n)],
                table.at[pl.ds(landing + r, rows), pl.ds(g, n)],
                first + i,
                to_band,
                patch,
            )
            for i, (r, rows, g, n) in enumerate(cuts)
        ]

    g_north = halo(0, 6, G_NORTH, north_band)
    g_south = halo(2, 4, G_SOUTH, south_band)
    g_west = remote(table.at[pl.ds(0, 4), 0], table.at[8, pl.ds(4, 4)], G_WEST, band, west)
    g_east = remote(table.at[pl.ds(0, 4), groups - 1], table.at[8, pl.ds(0, 4)], G_EAST, band, east)
    g_north_on = [
        remote(table.at[pl.ds(4, 2), 0], table.at[8, pl.ds(10, 2)], G_FORWARD, band, west),
        remote(table.at[pl.ds(4, 2), groups - 1], table.at[8, pl.ds(8, 2)], G_FORWARD + 1, band, east),
    ]
    g_south_on = [
        remote(table.at[pl.ds(6, 2), 0], table.at[8, pl.ds(14, 2)], G_FORWARD + 2, band, west),
        remote(table.at[pl.ds(6, 2), groups - 1], table.at[8, pl.ds(12, 2)], G_FORWARD + 3, band, east),
    ]

    chunk = BORDER // 2

    def near_copies(own, near, first):
        rows = own.at[pl.ds(0, BORDER)]
        flat = [remote(rows, near.at[3], first, band, west), remote(rows, near.at[2], first + 1, band, east)]
        norths, souths, norths_on, souths_on = [], [], [], []
        for c in range(2):
            n = first + 2 + 6 * c
            part = pl.ds(c * chunk, chunk)
            norths.append(remote(own.at[part], near.at[1, part], n, north_band, patch))
            souths.append(remote(own.at[part], near.at[0, part], n + 1, south_band, patch))
            norths_on += [
                remote(near.at[0, part], near.at[5, part], n + 2, band, west),
                remote(near.at[0, part], near.at[4, part], n + 3, band, east),
            ]
            souths_on += [
                remote(near.at[1, part], near.at[7, part], n + 4, band, west),
                remote(near.at[1, part], near.at[6, part], n + 5, band, east),
            ]
        return norths, souths, flat, norths_on, souths_on

    def pass_chunk(c, norths, souths, flat, norths_on, souths_on):
        two = slice(2 * c, 2 * c + 2)
        pass_on(norths[c : c + 1], souths[c : c + 1], norths_on[two], souths_on[two])

    def when_all(condition, copies, method):
        @pl.when(condition)
        def _():
            for copy in copies:
                getattr(copy, method)()

    def start_sides(north, south, flat):
        when_all(has_north, north, "start")
        when_all(has_south, south, "start")
        for copy in flat:
            copy.start()

    def pass_on(from_south, from_north, north_on, south_on):
        when_all(has_north, from_north, "wait_recv")
        when_all(has_north, north_on, "start")
        when_all(has_south, from_south, "wait_recv")
        when_all(has_south, south_on, "start")

    def arrived(flat, north_on, south_on):
        for copy in flat:
            copy.wait_recv()
        when_all(has_north, north_on, "wait_recv")
        when_all(has_south, south_on, "wait_recv")

    def sent(north, south, flat, north_on, south_on):
        when_all(has_north, north, "wait_send")
        when_all(has_south, south, "wait_send")
        for copy in flat:
            copy.wait_send()
        when_all(has_north, north_on, "wait_send")
        when_all(has_south, south_on, "wait_send")

    def loop(count, step, unroll=1):
        def one(i, carry):
            step(i)
            return carry

        lax.fori_loop(0, count, one, 0, unroll=unroll)

    def at(i):
        return pl.ds(pl.multiple_of(i * ROWS, ROWS), ROWS)

    grid_steps = lat * lon // ROWS

    def grid_rows(i):
        return grid[pl.ds(i * half_lat, half_lat)].reshape(ROWS, latent)

    need("grid", "e0")

    def send_step(i):
        rows = dot(grid_rows(i), encw[0]).astype(BF)
        table[pl.ds(i * half_lat, half_lat)] = rows.reshape(half_lat, groups, 16, latent)

    send_step(0)
    pl.semaphore_wait(barrier, bands - 1 + len(greeted))
    when_all(has_north, g_north, "start")
    for i in range(1, grid_steps):
        send_step(i)
    when_all(has_south, g_south, "start")
    g_west.start()
    g_east.start()

    need("e78")

    def self_step(i):
        rows = grid_rows(i)
        hidden = silu(dot(rows, encw[7])).astype(BF)
        gnext[at(i)] = (rows.astype(F32) + layer_norm(dot(hidden, encw[8]))).astype(BF)

    loop(grid_steps, self_step)
    need("mesh", "e12")
    mrecv[...] = dot(mesh[...], encw[1]).astype(BF)
    need("e36")
    base[...] = dot(mesh[...], encw[4])
    pass_on(g_north[:2], g_south[:2], g_north_on, g_south_on)

    width = lon + 2 * HALO

    def grid_place(s):
        i = jnp.zeros_like(s)
        for k in range(1, lat + 2 * HALO):
            i = i + (s >= k * width).astype(jnp.int32)
        j = s - i * width
        north, south = i < HALO, i >= lat + HALO
        line = jnp.where(north, i + 4, jnp.where(south, i, i - 2))
        inner = line * lon + j - HALO
        left = jnp.where(north, i + 8, jnp.where(south, i + 6, i - 2)) * 16 + j + 14
        right = jnp.where(north, i + 10, jnp.where(south, i + 8, i + 2)) * 16 + j - (lon + HALO)
        edge = 8 * lon + jnp.where(j < HALO, left, right)
        return jnp.where((j < HALO) | (j >= lon + HALO), edge, inner)

    shift = patches.bit_length() - 1

    def node_place(s, coarse):
        q = s >> 8
        slot = jnp.zeros_like(q)
        for name, number in ((0, 4), (2, 5), (3, 2), (5, 3), (6, 6), (7, 1), (8, 7)):
            slot = jnp.where(q == name, number, slot)
        distant_rows = bands * patches * COARSE_DEV
        shifted = jnp.where(slot >= 4, distant_rows, 0) + slot * BORDER if coarse else slot * BORDER
        near = jnp.where(q == 4, s - 4 * nodes, nodes + shifted + (s & (nodes - 1)))
        if not coarse:
            return near
        c = s - 9 * nodes
        device = c >> 4
        distant = ((device & (patches - 1)) * bands + (device >> shift)) * COARSE_DEV + (c & (COARSE_DEV - 1))
        return jnp.where(c < 0, near, distant + nodes + 4 * BORDER)

    def dec_columns(k, i):
        rows = [dsend[k, pl.ds(i * half_lat + r, 1), :] for r in range(half_lat)]
        return columns_of(node_place(jnp.concatenate(rows, axis=1), False))

    need("gs", "gr", "gf")

    def enc_own(i):
        place = columns_of(grid_place(gsend[:, at(i)]))
        cols_g[at(i)] = place
        recv = columns_of(grecv[:, at(i)])
        left = jnp.concatenate([gfeat[at(i)], pick(place, 0, 4 * lon), pick(recv, 0, nodes)], axis=1)
        right = jnp.concatenate([encw[2], table[0:4].reshape(4 * lon, latent), mrecv[...]], axis=0)
        pre_e[at(i)] = dot(left, right)

    loop(gfeat.shape[0] // ROWS, enc_own)
    need("ps", "pr", "ds")

    def proc_place(i):
        cols_p[at(i)] = columns_of(node_place(psend[:, at(i)], True))

    loop(pfeat.shape[0] // ROWS, proc_place)

    def dec_place(i):
        for k in range(3):
            cols_d[k, at(i)] = dec_columns(k, i)

    loop(grid_steps, dec_place)
    need("d")

    def dec_grid(i):
        recv_d[at(i)] = dot(gnext[at(i)], decw[1]).astype(BF)

    loop(grid_steps, dec_grid)
    need("blocks", "p2", "pf", "p01", "df")

    arrived([g_west, g_east], g_north_on, g_south_on)
    when_all(has_south, g_north[2:3], "wait_recv")
    when_all(has_north, g_south[2:3], "wait_recv")

    def enc_first(i):
        place = cols_g[at(i)]
        left = jnp.concatenate([pick(place, n * lon, lon) for n in (4, 6, 8)], axis=1)
        right = jnp.concatenate([table[n].reshape(lon, latent) for n in (4, 6, 8)], axis=0)
        pre_e[at(i)] = pre_e[at(i)] + dot(left, right)

    loop(gfeat.shape[0] // ROWS, enc_first)
    when_all(has_south, g_north[3:], "wait_recv")
    when_all(has_north, g_south[3:], "wait_recv")
    total[...] = jnp.zeros_like(total)
    live = blocks[patch, band] * 128

    def enc_edges(i):
        place = cols_g[at(i)]
        left = jnp.concatenate([pick(place, n * lon, lon) for n in (5, 7)], axis=1)
        right = jnp.concatenate([table[n].reshape(lon, latent) for n in (5, 7)], axis=0)
        before = pre_e[at(i)] + dot(left, right)
        message = layer_norm(dot(silu(before).astype(BF), encw[3])).astype(BF)
        edge = lax.broadcasted_iota(jnp.int32, (1, ROWS), 1) + i * ROWS
        receiver = jnp.where(edge < live, grecv[:, at(i)], -1)
        total[...] += dot(scatter(receiver, nodes), message)

    loop(gfeat.shape[0] // ROWS, enc_edges, 2)

    def mesh_step(current, weights, first):
        before = base[...] + dot(total[...].astype(BF), weights[first + 1])
        hidden = silu(before).astype(BF)
        return (current.astype(F32) + layer_norm(dot(hidden, weights[first + 2]))).astype(BF)

    mnext[...] = mesh_step(mesh[...], encw, 4)
    sent(g_north, g_south, [g_west, g_east], g_north_on, g_south_on)

    pown[...] = dot(mnext[...], procw[0]).astype(BF)
    pcoarse[patch, band] = pown[nodes - COARSE_DEV :]
    p_near = near_copies(pown, pnear, P_FIRST)
    columns = []
    for k in range(1, bands):
        own = pcoarse.at[patch, band]
        there = pcoarse.at[patch, lax.rem(band + bands - k, bands)]
        columns.append(
            (
                remote(own, own, C_BASE + k, lax.rem(band + k, bands), patch),
                remote(there, there, C_BASE + k, lax.rem(band + k, bands), patch),
            )
        )
    for out_copy, _ in columns:
        out_copy.start()
    start_sides(*p_near[:3])
    precv_rows[...] = dot(mnext[...], procw[1]).astype(BF)
    need("p36")
    base[...] = dot(mnext[...], procw[4])

    def proc_own(i):
        recv = columns_of(precv[:, at(i)])
        left = jnp.concatenate([pfeat[at(i)], pick(cols_p[at(i)], 0, nodes), pick(recv, 0, nodes)], axis=1)
        right = jnp.concatenate([procw[2], pown[...], precv_rows[...]], axis=0)
        pre_e[at(i)] = dot(left, right)

    def dec_update(i):
        upd[at(i)] = dot(gnext[at(i)], decw[4])

    loop(grid_steps, dec_update)

    for _, in_copy in columns:
        in_copy.wait_recv()
    cores = 2
    count = patches // cores
    first_id = C_BASE + bands
    mate = patch + 1 - 2 * lax.rem(patch, 2)
    across, over = [], []
    for k in range(count):
        column = lax.rem(patch + patches - cores * k, patches)
        mate_column = lax.rem(mate + patches - cores * k, patches)
        src, got = pcoarse.at[column], pcoarse.at[mate_column]
        over.append(
            (remote(src, src, first_id + count + k, band, mate), remote(got, got, first_id + count + k, band, mate))
        )
        if k:
            to = lax.rem(patch + cores * k, patches)
            own = pcoarse.at[patch]
            across.append((remote(own, own, first_id + k, band, to), remote(src, src, first_id + k, band, to)))
    for out_copy, _ in across:
        out_copy.start()
    over[0][0].start()
    pass_chunk(0, *p_near)
    half = pfeat.shape[0] // ROWS // 2
    loop(half, proc_own)
    pass_chunk(1, *p_near)
    for k, (_, in_copy) in enumerate(across):
        in_copy.wait_recv()
        over[k + 1][0].start()

    loop(pfeat.shape[0] // ROWS - half, lambda i: proc_own(i + half))
    for _, in_copy in over:
        in_copy.wait_recv()
    sides = 4 * BORDER
    distant_rows = bands * patches * COARSE_DEV

    def proc_first(i):
        right = jnp.concatenate(
            [pnear[0:4].reshape(sides, latent), pcoarse[...].reshape(distant_rows, latent)], axis=0
        )
        pre_e[at(i)] = pre_e[at(i)] + dot(pick(cols_p[at(i)], nodes, sides + distant_rows), right)

    for copy in p_near[2]:
        copy.wait_recv()
    loop(pfeat.shape[0] // ROWS, proc_first)
    arrived([], *p_near[3:])

    total[...] = jnp.zeros_like(total)

    def proc_edges(i):
        corners = pick(cols_p[at(i)], nodes + sides + distant_rows, sides)
        before = pre_e[at(i)] + dot(corners, pnear[4:8].reshape(sides, latent))
        message = layer_norm(dot(silu(before).astype(BF), procw[3])).astype(BF)
        total[...] += dot(scatter(precv[:, at(i)], nodes), message)

    loop(pfeat.shape[0] // ROWS, proc_edges, 2)
    last = mesh_step(mnext[...], procw, 4)
    for out_copy, _ in columns + across + over:
        out_copy.wait_send()
    sent(*p_near)

    down[...] = dot(last, decw[0]).astype(BF)
    d_near = near_copies(down, dnear, D_FIRST)
    start_sides(*d_near[:3])

    def dec_own(i):
        recv = recv_d[at(i)].astype(F32)
        right = jnp.concatenate([decw[2], down[...]], axis=0)
        for k in range(3):
            rows = dfeat[k, pl.ds(i * half_lat, half_lat)].reshape(ROWS, latent)
            left = jnp.concatenate([rows, pick(cols_d[k, at(i)], 0, nodes)], axis=1)
            pre_d[k, at(i)] = dot(left, right) + recv

    dec_own(0)
    pass_chunk(0, *d_near)
    for i in range(1, grid_steps):
        dec_own(i)
    pass_chunk(1, *d_near)
    for copy in d_near[2]:
        copy.wait_recv()

    def dec_first(i):
        for k in range(3):
            left = pick(cols_d[k, at(i)], nodes, sides)
            pre_d[k, at(i)] = pre_d[k, at(i)] + dot(left, dnear[0:4].reshape(sides, latent))

    loop(grid_steps, dec_first)
    arrived([], *d_near[3:])

    def dec_edges(i):
        near = dnear[4:8].reshape(sides, latent)
        summed = jnp.zeros((ROWS, latent), F32)
        for k in range(3):
            before = pre_d[k, at(i)] + dot(pick(cols_d[k, at(i)], nodes + sides, sides), near)
            message = layer_norm(dot(silu(before).astype(BF), decw[3])).astype(BF)
            summed = summed + message.astype(F32)
        hidden = silu(upd[at(i)] + dot(summed.astype(BF), decw[5])).astype(BF)
        rows = (gnext[at(i)].astype(F32) + layer_norm(dot(hidden, decw[6]))).astype(BF)
        result[pl.ds(i * half_lat, half_lat)] = rows.reshape(half_lat, lon, latent)

    stores = []
    for i in range(grid_steps):
        dec_edges(i)
        part = pl.ds(i * half_lat, half_lat)
        stores.append(pltpu.make_async_copy(result.at[part], out.at[part], out_sem.at[i]))
        stores[-1].start()
    sent(*d_near)
    for copy in stores:
        copy.wait()


def solution(mesh):
    bands, patches = mesh.shape["band"], mesh.shape["patch"]

    def shards(grid, mesh_state, gfeat, gsend, grecv, blocks, pfeat, psend, precv, dfeat, dsend, encw, procw, decw):
        lat, lon, latent = grid.shape
        nodes = mesh_state.shape[2]
        edges, pedges = gfeat.shape[2], pfeat.shape[2]
        cells = lat * lon
        any_spec = pl.BlockSpec(memory_space=pl.ANY)
        vmem = pltpu.VMEM
        copies = C_BASE + bands + patches
        return pl.pallas_call(
            functools.partial(body, bands, patches),
            out_shape=jax.ShapeDtypeStruct(grid.shape, BF),
            in_specs=[any_spec] * 14,
            out_specs=any_spec,
            scratch_shapes=[
                vmem(grid.shape, BF),
                vmem((nodes, latent), BF),
                vmem((edges, latent), BF),
                vmem((1, edges), jnp.int32),
                vmem((1, edges), jnp.int32),
                vmem((pedges, latent), BF),
                vmem((1, pedges), jnp.int32),
                vmem((1, pedges), jnp.int32),
                vmem(dfeat.shape, BF),
                vmem(dsend.shape, jnp.int32),
                vmem(encw.shape, BF),
                vmem(procw.shape, BF),
                vmem(decw.shape, BF),
                vmem((9, lon // 16, 16, latent), BF),
                vmem((nodes, latent), BF),
                vmem((cells, latent), BF),
                vmem((max(edges, pedges), latent), F32),
                vmem((3, cells, latent), F32),
                vmem((cells, latent), F32),
                vmem((nodes, latent), F32),
                vmem((edges, 128), jnp.int16),
                vmem((pedges, 128), jnp.int16),
                vmem((3, cells, 128), jnp.int16),
                pltpu.SMEM((patches, bands), jnp.int32),
                vmem((nodes, latent), F32),
                vmem((nodes, latent), BF),
                vmem((nodes, latent), BF),
                vmem((8, BORDER, latent), BF),
                vmem((patches, bands, COARSE_DEV, latent), BF),
                vmem((nodes, latent), BF),
                vmem((cells, latent), BF),
                vmem((nodes, latent), BF),
                vmem((8, BORDER, latent), BF),
                vmem(grid.shape, BF),
                pltpu.SemaphoreType.DMA((19,)),
                pltpu.SemaphoreType.DMA((2,)),
                pltpu.SemaphoreType.DMA((copies,)),
                pltpu.SemaphoreType.DMA((copies,)),
            ],
            compiler_params=pltpu.CompilerParams(
                collective_id=0, has_side_effects=True, vmem_limit_bytes=62 * 1024 * 1024
            ),
            cost_estimate=pl.CostEstimate(flops=24 * 10**9, bytes_accessed=24 * 10**6, transcendentals=5 * 10**6),
        )(grid, mesh_state, gfeat, gsend, grecv, blocks.T, pfeat, psend, precv, dfeat, dsend, encw, procw, decw)

    placed = (
        P("band", "patch", None),
        P("band", "patch", None, None),
        P("band", "patch", None, None),
        P("band", "patch", None),
        P("band", "patch", None),
        P(),
        P("band", "patch", None, None),
        P("band", "patch", None),
        P("band", "patch", None),
        P(None, "band", "patch", None),
        P(None, "band", "patch"),
        P(),
        P(),
        P(),
    )
    return jax.shard_map(
        shards, mesh=mesh, in_specs=placed, out_specs=P("band", "patch", None), check_vma=False
    )
```

```python
import functools

import jax
import jax.numpy as jnp
from jax import lax
from jax.experimental import pallas as pl
from jax.experimental.pallas import tpu as pltpu
from jax.sharding import PartitionSpec as P

MESH = pl.DeviceIdType.MESH
COARSE_DEV = 16
HALO = 2
BORDER = 64
EPSILON = 1e-05
BF = jnp.bfloat16
F32 = jnp.float32
ROWS = 512

G_NORTH, G_SOUTH, G_WEST, G_EAST = 0, 4, 8, 9
G_FORWARD = 10
P_FIRST, D_FIRST = 14, 28
C_BASE = 42


def dot(a, b):
    return jnp.dot(a, b, preferred_element_type=F32)


def silu(v):
    half = 0.5 * v
    return half + half * jnp.tanh(half)


def layer_norm(v):
    centred = v - jnp.mean(v, axis=-1, keepdims=True)
    spread = jnp.mean(centred * centred, axis=-1, keepdims=True)
    return centred * lax.rsqrt(spread + EPSILON)


def columns_of(row):
    n = row.shape[1]
    wide = jnp.broadcast_to(row.astype(F32), (128, n)).T
    return wide.astype(jnp.int32).astype(jnp.int16)


def pick(columns, first, count):
    lane = lax.broadcasted_iota(jnp.int16, columns.shape, 1)
    parts = []
    for start in range(first, first + count, 128):
        hit = columns == lane + jnp.int16(start)
        parts.append(jnp.where(hit, BF(1), BF(0)))
    return jnp.concatenate(parts, axis=1) if len(parts) > 1 else parts[0]


def scatter(row, nodes):
    hit = lax.broadcasted_iota(jnp.int32, (nodes, row.shape[1]), 0) == row
    return jnp.where(hit, 1.0, 0.0).astype(BF)


def body(
    bands,
    patches,
    grid_in,
    mesh_in,
    gfeat_in,
    gsend_in,
    grecv_in,
    blocks_in,
    pfeat_in,
    psend_in,
    precv_in,
    dfeat_in,
    dsend_in,
    encw_in,
    procw_in,
    decw_in,
    hidden_out,
    gnext_out,
    grid,
    mesh,
    gfeat,
    gsend,
    grecv,
    pfeat,
    psend,
    precv,
    dfeat,
    dsend,
    encw,
    procw,
    decw,
    table,
    mrecv,
    gnext,
    pre_e,
    pre_d,
    upd,
    base,
    cols_g,
    cols_p,
    cols_d,
    blocks,
    total,
    mnext,
    pown,
    pnear,
    pcoarse,
    precv_rows,
    recv_d,
    down,
    dnear,
    result,
    in_sem,
    out_sem,
    send_sem,
    recv_sem,
):
    band, patch = lax.axis_index("band"), lax.axis_index("patch")
    has_north, has_south = band > 0, band < bands - 1
    west, east = lax.rem(patch + patches - 1, patches), lax.rem(patch + 1, patches)
    lat, lon, latent = grid.shape
    nodes = mesh.shape[0]
    half_lat = ROWS // lon

    loads = {}

    def load(name, src, dst):
        copy = pltpu.make_async_copy(src, dst, in_sem.at[len(loads)])
        copy.start()
        loads[name] = copy

    load("e0", encw_in.at[0], encw.at[0])
    load("grid", grid_in, grid)
    load("e78", encw_in.at[pl.ds(7, 2)], encw.at[pl.ds(7, 2)])
    load("mesh", mesh_in.at[0, 0], mesh)
    load("e12", encw_in.at[pl.ds(1, 2)], encw.at[pl.ds(1, 2)])
    load("gs", gsend_in.at[0], gsend)
    load("gr", grecv_in.at[0], grecv)
    load("ps", psend_in.at[0], psend)
    load("pr", precv_in.at[0], precv)
    load("ds", dsend_in, dsend)
    load("blocks", blocks_in, blocks)
    load("gf", gfeat_in.at[0, 0], gfeat)
    load("p2", procw_in.at[2], procw.at[2])
    load("pf", pfeat_in.at[0, 0], pfeat)
    load("e36", encw_in.at[pl.ds(3, 4)], encw.at[pl.ds(3, 4)])
    load("p01", procw_in.at[pl.ds(0, 2)], procw.at[pl.ds(0, 2)])
    load("d", decw_in, decw)
    load("df", dfeat_in, dfeat)
    load("p36", procw_in.at[pl.ds(3, 4)], procw.at[pl.ds(3, 4)])

    def need(*names):
        for name in names:
            loads[name].wait()

    barrier = pltpu.get_barrier_semaphore()
    for k in range(1, bands):
        pl.semaphore_signal(
            barrier, inc=1, device_id={"band": lax.rem(band + k, bands), "patch": patch}, device_id_type=MESH
        )
    greeted = [k for k in range(1, patches) if k in (1, patches - 1) or k % 2 == 0]
    for k in greeted:
        pl.semaphore_signal(
            barrier, inc=1, device_id={"band": band, "patch": lax.rem(patch + k, patches)}, device_id_type=MESH
        )

    def remote(src, dst, number, to_band, to_patch):
        return pltpu.make_async_remote_copy(
            src_ref=src,
            dst_ref=dst,
            send_sem=send_sem.at[number],
            recv_sem=recv_sem.at[number],
            device_id={"band": to_band, "patch": to_patch},
            device_id_type=MESH,
        )

    @pl.when(jnp.logical_not(has_north))
    def _():
        table[4:6] = jnp.zeros_like(table[4:6])
        table[8, 8:12] = jnp.zeros_like(table[8, 8:12])
        pnear[0] = jnp.zeros_like(pnear[0])
        pnear[4:6] = jnp.zeros_like(pnear[4:6])
        dnear[0] = jnp.zeros_like(dnear[0])
        dnear[4:6] = jnp.zeros_like(dnear[4:6])

    @pl.when(jnp.logical_not(has_south))
    def _():
        table[6:8] = jnp.zeros_like(table[6:8])
        table[8, 12:16] = jnp.zeros_like(table[8, 12:16])
        pnear[1] = jnp.zeros_like(pnear[1])
        pnear[6:8] = jnp.zeros_like(pnear[6:8])
        dnear[1] = jnp.zeros_like(dnear[1])
        dnear[6:8] = jnp.zeros_like(dnear[6:8])

    groups = lon // 16
    north_band, south_band = lax.rem(band + bands - 1, bands), lax.rem(band + 1, bands)
    cuts = ((0, 2, 0, 1), (0, 2, groups - 1, 1), (0, 1, 1, groups - 2), (1, 1, 1, groups - 2))

    def halo(start, landing, first, to_band):
        return [
            remote(
                table.at[pl.ds(start + r, rows), pl.ds(g, n)],
                table.at[pl.ds(landing + r, rows), pl.ds(g, n)],
                first + i,
                to_band,
                patch,
            )
            for i, (r, rows, g, n) in enumerate(cuts)
        ]

    g_north = halo(0, 6, G_NORTH, north_band)
    g_south = halo(2, 4, G_SOUTH, south_band)
    g_west = remote(table.at[pl.ds(0, 4), 0], table.at[8, pl.ds(4, 4)], G_WEST, band, west)
    g_east = remote(table.at[pl.ds(0, 4), groups - 1], table.at[8, pl.ds(0, 4)], G_EAST, band, east)
    g_north_on = [
        remote(table.at[pl.ds(4, 2), 0], table.at[8, pl.ds(10, 2)], G_FORWARD, band, west),
        remote(table.at[pl.ds(4, 2), groups - 1], table.at[8, pl.ds(8, 2)], G_FORWARD + 1, band, east),
    ]
    g_south_on = [
        remote(table.at[pl.ds(6, 2), 0], table.at[8, pl.ds(14, 2)], G_FORWARD + 2, band, west),
        remote(table.at[pl.ds(6, 2), groups - 1], table.at[8, pl.ds(12, 2)], G_FORWARD + 3, band, east),
    ]

    chunk = BORDER // 2

    def near_copies(own, near, first):
        rows = own.at[pl.ds(0, BORDER)]
        flat = [remote(rows, near.at[3], first, band, west), remote(rows, near.at[2], first + 1, band, east)]
        norths, souths, norths_on, souths_on = [], [], [], []
        for c in range(2):
            n = first + 2 + 6 * c
            part = pl.ds(c * chunk, chunk)
            norths.append(remote(own.at[part], near.at[1, part], n, north_band, patch))
            souths.append(remote(own.at[part], near.at[0, part], n + 1, south_band, patch))
            norths_on += [
                remote(near.at[0, part], near.at[5, part], n + 2, band, west),
                remote(near.at[0, part], near.at[4, part], n + 3, band, east),
            ]
            souths_on += [
                remote(near.at[1, part], near.at[7, part], n + 4, band, west),
                remote(near.at[1, part], near.at[6, part], n + 5, band, east),
            ]
        return norths, souths, flat, norths_on, souths_on

    def pass_chunk(c, norths, souths, flat, norths_on, souths_on):
        two = slice(2 * c, 2 * c + 2)
        pass_on(norths[c : c + 1], souths[c : c + 1], norths_on[two], souths_on[two])

    def when_all(condition, copies, method):
        @pl.when(condition)
        def _():
            for copy in copies:
                getattr(copy, method)()

    def start_sides(north, south, flat):
        when_all(has_north, north, "start")
        when_all(has_south, south, "start")
        for copy in flat:
            copy.start()

    def pass_on(from_south, from_north, north_on, south_on):
        when_all(has_north, from_north, "wait_recv")
        when_all(has_north, north_on, "start")
        when_all(has_south, from_south, "wait_recv")
        when_all(has_south, south_on, "start")

    def arrived(flat, north_on, south_on):
        for copy in flat:
            copy.wait_recv()
        when_all(has_north, north_on, "wait_recv")
        when_all(has_south, south_on, "wait_recv")

    def sent(north, south, flat, north_on, south_on):
        when_all(has_north, north, "wait_send")
        when_all(has_south, south, "wait_send")
        for copy in flat:
            copy.wait_send()
        when_all(has_north, north_on, "wait_send")
        when_all(has_south, south_on, "wait_send")

    def loop(count, step, unroll=1):
        def one(i, carry):
            step(i)
            return carry

        lax.fori_loop(0, count, one, 0, unroll=unroll)

    def at(i):
        return pl.ds(pl.multiple_of(i * ROWS, ROWS), ROWS)

    grid_steps = lat * lon // ROWS

    def grid_rows(i):
        return grid[pl.ds(i * half_lat, half_lat)].reshape(ROWS, latent)

    need("grid", "e0")

    def send_step(i):
        rows = dot(grid_rows(i), encw[0]).astype(BF)
        table[pl.ds(i * half_lat, half_lat)] = rows.reshape(half_lat, groups, 16, latent)

    send_step(0)
    pl.semaphore_wait(barrier, bands - 1 + len(greeted))
    when_all(has_north, g_north, "start")
    for i in range(1, grid_steps):
        send_step(i)
    when_all(has_south, g_south, "start")
    g_west.start()
    g_east.start()

    need("e78")

    def self_step(i):
        rows = grid_rows(i)
        hidden = silu(dot(rows, encw[7])).astype(BF)
        gnext[at(i)] = (rows.astype(F32) + layer_norm(dot(hidden, encw[8]))).astype(BF)

    loop(grid_steps, self_step)
    keep = pltpu.make_async_copy(gnext, gnext_out, out_sem.at[grid_steps])
    keep.start()
    need("mesh", "e12")
    mrecv[...] = dot(mesh[...], encw[1]).astype(BF)
    need("e36")
    base[...] = dot(mesh[...], encw[4])
    pass_on(g_north[:2], g_south[:2], g_north_on, g_south_on)

    width = lon + 2 * HALO

    def grid_place(s):
        i = jnp.zeros_like(s)
        for k in range(1, lat + 2 * HALO):
            i = i + (s >= k * width).astype(jnp.int32)
        j = s - i * width
        north, south = i < HALO, i >= lat + HALO
        line = jnp.where(north, i + 4, jnp.where(south, i, i - 2))
        inner = line * lon + j - HALO
        left = jnp.where(north, i + 8, jnp.where(south, i + 6, i - 2)) * 16 + j + 14
        right = jnp.where(north, i + 10, jnp.where(south, i + 8, i + 2)) * 16 + j - (lon + HALO)
        edge = 8 * lon + jnp.where(j < HALO, left, right)
        return jnp.where((j < HALO) | (j >= lon + HALO), edge, inner)

    shift = patches.bit_length() - 1

    def node_place(s, coarse):
        q = s >> 8
        slot = jnp.zeros_like(q)
        for name, number in ((0, 4), (2, 5), (3, 2), (5, 3), (6, 6), (7, 1), (8, 7)):
            slot = jnp.where(q == name, number, slot)
        distant_rows = bands * patches * COARSE_DEV
        shifted = jnp.where(slot >= 4, distant_rows, 0) + slot * BORDER if coarse else slot * BORDER
        near = jnp.where(q == 4, s - 4 * nodes, nodes + shifted + (s & (nodes - 1)))
        if not coarse:
            return near
        c = s - 9 * nodes
        device = c >> 4
        distant = ((device & (patches - 1)) * bands + (device >> shift)) * COARSE_DEV + (c & (COARSE_DEV - 1))
        return jnp.where(c < 0, near, distant + nodes + 4 * BORDER)

    def dec_columns(k, i):
        rows = [dsend[k, pl.ds(i * half_lat + r, 1), :] for r in range(half_lat)]
        return columns_of(node_place(jnp.concatenate(rows, axis=1), False))

    need("gs", "gr", "gf")

    def enc_own(i):
        place = columns_of(grid_place(gsend[:, at(i)]))
        cols_g[at(i)] = place
        recv = columns_of(grecv[:, at(i)])
        left = jnp.concatenate([gfeat[at(i)], pick(place, 0, 4 * lon), pick(recv, 0, nodes)], axis=1)
        right = jnp.concatenate([encw[2], table[0:4].reshape(4 * lon, latent), mrecv[...]], axis=0)
        pre_e[at(i)] = dot(left, right)

    loop(gfeat.shape[0] // ROWS, enc_own)
    need("ps", "pr", "ds")

    def proc_place(i):
        cols_p[at(i)] = columns_of(node_place(psend[:, at(i)], True))

    loop(pfeat.shape[0] // ROWS, proc_place)

    need("blocks", "p2", "pf", "p01", "d", "df")

    arrived([g_west, g_east], g_north_on, g_south_on)
    when_all(has_south, g_north[2:3], "wait_recv")
    when_all(has_north, g_south[2:3], "wait_recv")

    def enc_first(i):
        place = cols_g[at(i)]
        left = jnp.concatenate([pick(place, n * lon, lon) for n in (4, 6, 8)], axis=1)
        right = jnp.concatenate([table[n].reshape(lon, latent) for n in (4, 6, 8)], axis=0)
        pre_e[at(i)] = pre_e[at(i)] + dot(left, right)

    loop(gfeat.shape[0] // ROWS, enc_first)
    when_all(has_south, g_north[3:], "wait_recv")
    when_all(has_north, g_south[3:], "wait_recv")
    total[...] = jnp.zeros_like(total)
    live = blocks[patch, band] * 128

    def enc_edges(i):
        place = cols_g[at(i)]
        left = jnp.concatenate([pick(place, n * lon, lon) for n in (5, 7)], axis=1)
        right = jnp.concatenate([table[n].reshape(lon, latent) for n in (5, 7)], axis=0)
        before = pre_e[at(i)] + dot(left, right)
        message = layer_norm(dot(silu(before).astype(BF), encw[3])).astype(BF)
        edge = lax.broadcasted_iota(jnp.int32, (1, ROWS), 1) + i * ROWS
        receiver = jnp.where(edge < live, grecv[:, at(i)], -1)
        total[...] += dot(scatter(receiver, nodes), message)

    loop(gfeat.shape[0] // ROWS, enc_edges, 2)

    def mesh_step(current, weights, first):
        before = base[...] + dot(total[...].astype(BF), weights[first + 1])
        hidden = silu(before).astype(BF)
        return (current.astype(F32) + layer_norm(dot(hidden, weights[first + 2]))).astype(BF)

    mnext[...] = mesh_step(mesh[...], encw, 4)
    sent(g_north, g_south, [g_west, g_east], g_north_on, g_south_on)

    pown[...] = dot(mnext[...], procw[0]).astype(BF)
    pcoarse[patch, band] = pown[nodes - COARSE_DEV :]
    p_near = near_copies(pown, pnear, P_FIRST)
    columns = []
    for k in range(1, bands):
        own = pcoarse.at[patch, band]
        there = pcoarse.at[patch, lax.rem(band + bands - k, bands)]
        columns.append(
            (
                remote(own, own, C_BASE + k, lax.rem(band + k, bands), patch),
                remote(there, there, C_BASE + k, lax.rem(band + k, bands), patch),
            )
        )
    for out_copy, _ in columns:
        out_copy.start()
    start_sides(*p_near[:3])
    precv_rows[...] = dot(mnext[...], procw[1]).astype(BF)
    need("p36")
    base[...] = dot(mnext[...], procw[4])

    def proc_own(i):
        recv = columns_of(precv[:, at(i)])
        left = jnp.concatenate([pfeat[at(i)], pick(cols_p[at(i)], 0, nodes), pick(recv, 0, nodes)], axis=1)
        right = jnp.concatenate([procw[2], pown[...], precv_rows[...]], axis=0)
        pre_e[at(i)] = dot(left, right)

    def dec_update(i):
        both = dot(gnext[at(i)], jnp.concatenate([decw[1], decw[4]], axis=1))
        recv_d[at(i)] = both[:, :latent].astype(BF)
        upd[at(i)] = both[:, latent:]

    loop(grid_steps, dec_update)

    for _, in_copy in columns:
        in_copy.wait_recv()
    cores = 2
    count = patches // cores
    first_id = C_BASE + bands
    mate = patch + 1 - 2 * lax.rem(patch, 2)
    across, over = [], []
    for k in range(count):
        column = lax.rem(patch + patches - cores * k, patches)
        mate_column = lax.rem(mate + patches - cores * k, patches)
        src, got = pcoarse.at[column], pcoarse.at[mate_column]
        over.append(
            (remote(src, src, first_id + count + k, band, mate), remote(got, got, first_id + count + k, band, mate))
        )
        if k:
            to = lax.rem(patch + cores * k, patches)
            own = pcoarse.at[patch]
            across.append((remote(own, own, first_id + k, band, to), remote(src, src, first_id + k, band, to)))
    for out_copy, _ in across:
        out_copy.start()
    over[0][0].start()
    pass_chunk(0, *p_near)
    half = pfeat.shape[0] // ROWS // 2
    loop(half, proc_own)
    pass_chunk(1, *p_near)
    for k, (_, in_copy) in enumerate(across):
        in_copy.wait_recv()
        over[k + 1][0].start()

    loop(pfeat.shape[0] // ROWS - half, lambda i: proc_own(i + half))
    for _, in_copy in over:
        in_copy.wait_recv()
    sides = 4 * BORDER
    distant_rows = bands * patches * COARSE_DEV

    def proc_first(i):
        right = jnp.concatenate(
            [pnear[0:4].reshape(sides, latent), pcoarse[...].reshape(distant_rows, latent)], axis=0
        )
        pre_e[at(i)] = pre_e[at(i)] + dot(pick(cols_p[at(i)], nodes, sides + distant_rows), right)

    for copy in p_near[2]:
        copy.wait_recv()
    loop(pfeat.shape[0] // ROWS, proc_first)
    arrived([], *p_near[3:])

    total[...] = jnp.zeros_like(total)

    def proc_edges(i):
        corners = pick(cols_p[at(i)], nodes + sides + distant_rows, sides)
        before = pre_e[at(i)] + dot(corners, pnear[4:8].reshape(sides, latent))
        message = layer_norm(dot(silu(before).astype(BF), procw[3])).astype(BF)
        total[...] += dot(scatter(precv[:, at(i)], nodes), message)

    loop(pfeat.shape[0] // ROWS, proc_edges, 2)
    last = mesh_step(mnext[...], procw, 4)
    for out_copy, _ in columns + across + over:
        out_copy.wait_send()
    sent(*p_near)

    down[...] = dot(last, decw[0]).astype(BF)
    d_near = near_copies(down, dnear, D_FIRST)
    start_sides(*d_near[:3])

    def dec_own(i):
        recv = recv_d[at(i)].astype(F32)
        right = jnp.concatenate([decw[2], down[...]], axis=0)
        for k in range(3):
            cols_d[k, at(i)] = dec_columns(k, i)
            rows = dfeat[k, pl.ds(i * half_lat, half_lat)].reshape(ROWS, latent)
            left = jnp.concatenate([rows, pick(cols_d[k, at(i)], 0, nodes)], axis=1)
            pre_d[k, at(i)] = dot(left, right) + recv

    dec_own(0)
    pass_chunk(0, *d_near)
    for i in range(1, grid_steps):
        dec_own(i)
    pass_chunk(1, *d_near)
    for copy in d_near[2]:
        copy.wait_recv()

    def dec_first(i):
        for k in range(3):
            left = pick(cols_d[k, at(i)], nodes, sides)
            pre_d[k, at(i)] = pre_d[k, at(i)] + dot(left, dnear[0:4].reshape(sides, latent))

    loop(grid_steps, dec_first)
    arrived([], *d_near[3:])

    def dec_edges(i):
        near = dnear[4:8].reshape(sides, latent)
        summed = jnp.zeros((ROWS, latent), F32)
        for k in range(3):
            before = pre_d[k, at(i)] + dot(pick(cols_d[k, at(i)], nodes + sides, sides), near)
            message = layer_norm(dot(silu(before).astype(BF), decw[3])).astype(BF)
            summed = summed + message.astype(F32)
        hidden = silu(upd[at(i)] + dot(summed.astype(BF), decw[5])).astype(BF)
        result[at(i)] = hidden

    stores = []
    for i in range(grid_steps):
        dec_edges(i)
        part = pl.ds(i * ROWS, ROWS)
        stores.append(pltpu.make_async_copy(result.at[part], hidden_out.at[part], out_sem.at[i]))
        stores[-1].start()
    sent(*d_near)
    keep.wait()
    for copy in stores:
        copy.wait()


def finish_body(hidden, current, weight, out):
    rows = current[...].astype(F32) + layer_norm(dot(hidden[...], weight[0]))
    out[0] = rows.astype(BF)


def solution(mesh):
    bands, patches = mesh.shape["band"], mesh.shape["patch"]

    def shards(grid, mesh_state, gfeat, gsend, grecv, blocks, pfeat, psend, precv, dfeat, dsend, encw, procw, decw):
        lat, lon, latent = grid.shape
        nodes = mesh_state.shape[2]
        edges, pedges = gfeat.shape[2], pfeat.shape[2]
        cells = lat * lon
        any_spec = pl.BlockSpec(memory_space=pl.ANY)
        vmem = pltpu.VMEM
        copies = C_BASE + bands + patches
        hidden, current = pl.pallas_call(
            functools.partial(body, bands, patches),
            out_shape=[jax.ShapeDtypeStruct((cells, latent), BF)] * 2,
            in_specs=[any_spec] * 14,
            out_specs=[any_spec] * 2,
            scratch_shapes=[
                vmem(grid.shape, BF),
                vmem((nodes, latent), BF),
                vmem((edges, latent), BF),
                vmem((1, edges), jnp.int32),
                vmem((1, edges), jnp.int32),
                vmem((pedges, latent), BF),
                vmem((1, pedges), jnp.int32),
                vmem((1, pedges), jnp.int32),
                vmem(dfeat.shape, BF),
                vmem(dsend.shape, jnp.int32),
                vmem(encw.shape, BF),
                vmem(procw.shape, BF),
                vmem(decw.shape, BF),
                vmem((9, lon // 16, 16, latent), BF),
                vmem((nodes, latent), BF),
                vmem((cells, latent), BF),
                vmem((max(edges, pedges), latent), F32),
                vmem((3, cells, latent), F32),
                vmem((cells, latent), F32),
                vmem((nodes, latent), F32),
                vmem((edges, 128), jnp.int16),
                vmem((pedges, 128), jnp.int16),
                vmem((3, cells, 128), jnp.int16),
                pltpu.SMEM((patches, bands), jnp.int32),
                vmem((nodes, latent), F32),
                vmem((nodes, latent), BF),
                vmem((nodes, latent), BF),
                vmem((8, BORDER, latent), BF),
                vmem((patches, bands, COARSE_DEV, latent), BF),
                vmem((nodes, latent), BF),
                vmem((cells, latent), BF),
                vmem((nodes, latent), BF),
                vmem((8, BORDER, latent), BF),
                vmem((cells, latent), BF),
                pltpu.SemaphoreType.DMA((19,)),
                pltpu.SemaphoreType.DMA((cells // ROWS + 1,)),
                pltpu.SemaphoreType.DMA((copies,)),
                pltpu.SemaphoreType.DMA((copies,)),
            ],
            compiler_params=pltpu.CompilerParams(
                collective_id=0, has_side_effects=True, vmem_limit_bytes=62 * 1024 * 1024
            ),
            cost_estimate=pl.CostEstimate(flops=24 * 10**9, bytes_accessed=24 * 10**6, transcendentals=5 * 10**6),
        )(grid, mesh_state, gfeat, gsend, grecv, blocks.T, pfeat, psend, precv, dfeat, dsend, encw, procw, decw)
        rows_spec = pl.BlockSpec((lon, latent), lambda i: (i, 0))
        return pl.pallas_call(
            finish_body,
            grid=(lat,),
            out_shape=jax.ShapeDtypeStruct(grid.shape, BF),
            in_specs=[rows_spec, rows_spec, pl.BlockSpec((1, latent, latent), lambda i: (6, 0, 0))],
            out_specs=pl.BlockSpec((1, lon, latent), lambda i: (i, 0, 0)),
            compiler_params=pltpu.CompilerParams(vmem_limit_bytes=62 * 1024 * 1024),
            cost_estimate=pl.CostEstimate(
                flops=2 * cells * latent * latent, bytes_accessed=6 * cells * latent, transcendentals=cells
            ),
        )(hidden, current, decw)

    placed = (
        P("band", "patch", None),
        P("band", "patch", None, None),
        P("band", "patch", None, None),
        P("band", "patch", None),
        P("band", "patch", None),
        P(),
        P("band", "patch", None, None),
        P("band", "patch", None),
        P("band", "patch", None),
        P(None, "band", "patch", None),
        P(None, "band", "patch"),
        P(),
        P(),
        P(),
    )
    return jax.shard_map(
        shards, mesh=mesh, in_specs=placed, out_specs=P("band", "patch", None), check_vma=False
    )
```
